256 devices in a mesh: seq: 128 (over y_hi, x, z, core), head: 2 (over y_lo).
Axes of the slice: x: 4, y: 4 (y_hi: 2, y_lo: 2; y = y_hi * 2 + y_lo), z: 8, core: 2. Of those that a mesh axis runs over, the one named last changes fastest.
Arguments:
- queries: bfloat16 [16384, 2560], P('seq', 'head'), may hold values from -6 to 6
- keys: bfloat16 [16384, 2560], P('seq', 'head'), may hold values from -6 to 6
- values: bfloat16 [16384, 2560], P('seq', 'head'), may hold values from -6 to 6
- grad_out: bfloat16 [16384, 2560], P('seq', 'head'), may hold values from -6 to 6
- cache: bfloat16 [16384, 2560], P('seq', 'head'), may hold values from -6 to 6
- w_kv: bfloat16 [2, 2560, 2560], P(None, 'seq', 'head'), may hold values from -0.125 to 0.125
- doc_ids: int32 [16384], replicated, may hold values from 0 to 127, never falling along the last dimension, each value on 1 to 256 neighbouring positions
- routes: int32 [16384], replicated, may hold values from 0 to 127, as said below
Outputs:
- output: bfloat16 [16384, 2560], P('seq', 'head')
- grad_q: bfloat16 [16384, 2560], P('seq', 'head')
- grad_k: bfloat16 [16384, 2560], P('seq', 'head')
- grad_v: bfloat16 [16384, 2560], P('seq', 'head')
The draws below stay inside these ranges and needn't reach their ends.
Inputs may be any that keep to these rules, and one draw needn't show every extreme that they name: `routes`: each device's aligned block of 128 rows names every destination at most 2 times; in every draw some destination is named exactly 2 times by every block.
All inputs are finite; a program needn't handle non-finite values.
Results may differ from the reference program's by a relative error of at most 0.03.
Values may be sent and summed in bfloat16 or wider, within the bound.
A program may use at most 128 MiB of HBM per device.

```python
import math
import jax
import jax.numpy as jnp
import numpy as np
from jax import lax

H = 20
HD = 128
CW = 2560
SPAN = 2
S = 128
CACHE_DEV = 128
HF = 2560
TOKENS = 16384
CACHES = 16384
CAP = 2
DOC_MAX = 256
DOCS = 128
N_SEQ = 128


def draw_queries(key, part):
    drawn = jax.random.truncated_normal(jax.random.fold_in(key, 5), -6.0, 6.0, (TOKENS, HF), jnp.float32)
    return drawn.astype(jnp.bfloat16)


def draw_keys(key, part):
    drawn = jax.random.truncated_normal(jax.random.fold_in(key, 6), -6.0, 6.0, (TOKENS, HF), jnp.float32)
    return drawn.astype(jnp.bfloat16)


def draw_routes(key, part):
    hottest = jax.random.randint(jax.random.fold_in(key, 1), (), 0, N_SEQ)
    offsets = jax.random.randint(jax.random.fold_in(key, 2), (N_SEQ, 1), 0, N_SEQ - 1)
    ordinal = jnp.arange(CACHE_DEV, dtype=jnp.int32)[None, :] - CAP
    others = (offsets + jnp.maximum(ordinal, 0)) % (N_SEQ - 1)
    others = others + (others >= hottest).astype(jnp.int32)
    targets = jnp.where(ordinal < 0, hottest, others)
    shuffle_keys = jax.random.split(jax.random.fold_in(key, 3), N_SEQ)
    orders = jax.vmap(lambda one_key: jax.random.permutation(one_key, CACHE_DEV))(shuffle_keys)
    targets = jnp.take_along_axis(targets, orders, axis=1)
    return targets.reshape(-1).astype(jnp.int32)


def block_scale(rng, dims, cuts, least, largest):
    loudness = 1.0
    for position, parts in cuts:
        heights = jax.random.uniform(jax.random.fold_in(jax.random.fold_in(rng, 6), position), (parts,), jnp.float32, least / len(cuts), largest / len(cuts))
        loudness = loudness * jnp.repeat(jnp.exp(heights), dims[position] // parts).reshape((-1,) + (1,) * (len(dims) - 1 - position))
    return loudness


def length_profile(number_of, total, most, slope):
    portions = [(1 << 20) // math.isqrt(rank ** slope) + 1 for rank in range(2, number_of + 1)]
    surplus, counts = total - most - (number_of - 1), [1] * (number_of - 1)
    while surplus > 0:
        movable = [i for i in range(number_of - 1) if counts[i] < most]
        whole, budget = sum([portions[i] for i in movable]), surplus
        for i in movable:
            more = min(most - counts[i], max(1, budget * portions[i] // whole), surplus)
            counts[i] = counts[i] + more
            surplus = surplus - more
    return np.array([most] + counts)


def uneven(stream_key, amount, total, bound, slope):
    if amount == 2:
        one = jax.random.randint(stream_key, (), max(1, total - bound), min(bound, total - 1) + 1)
        return jnp.stack([one, total - one])
    lengths = jnp.asarray(length_profile(amount, total, bound, slope), jnp.int32)
    pairs = (amount - 1) // 2
    donor, receiver = lengths[1:1 + 2 * pairs:2], lengths[2:2 + 2 * pairs:2]
    margin = jnp.minimum(donor - 1, bound - receiver)
    shifted = jax.random.randint(jax.random.fold_in(stream_key, 1), (pairs,), 0, 1 << 20) % (margin + 1)
    lengths = lengths.at[1:1 + 2 * pairs:2].set(donor - shifted).at[2:2 + 2 * pairs:2].set(receiver + shifted)
    return lengths[jax.random.permutation(jax.random.fold_in(stream_key, 2), amount)]


def scatter_about(own_key, dims, width, bound, pieces=(), held_as=jnp.bfloat16):
    gain = block_scale(own_key, dims, pieces, -0.22, 0.18) if pieces else 1.0
    result = jax.random.normal(own_key, dims, jnp.float32) * width * gain
    return jnp.minimum(jnp.maximum(result, -bound), bound).astype(held_as)


def setup_inputs(seed: int = 0) -> dict:
    key_of = jax.random.split(jax.random.key(seed), 9)
    return {
        "queries": draw_queries(jax.random.fold_in(key_of[8], 71), 0),
        "keys": draw_keys(jax.random.fold_in(key_of[8], 71), 0),
        "values": scatter_about(key_of[2], (TOKENS, HF), 1.0, 6.0, ((0, 128), (1, 2))),
        "grad_out": scatter_about(key_of[3], (TOKENS, HF), 1.0, 6.0, ((0, 128), (1, 2))),
        "cache": scatter_about(key_of[4], (CACHES, CW), 1.0, 6.0, ((0, 128), (1, 2))),
        "w_kv": scatter_about(key_of[5], (2, CW, HF), CW ** -0.5, 0.125, ((1, 128), (2, 2))),
        "doc_ids": jnp.searchsorted(jnp.cumsum(uneven(key_of[6], DOCS, TOKENS, DOC_MAX, 0)), jnp.arange(TOKENS), side="right").astype(jnp.int32),
        "routes": draw_routes(jax.random.fold_in(key_of[8], 71), 0),
    }


def attend(queries, key_set, value_set, grad_out, allowed, head_count):
    seg_rows = queries.shape[0]
    key_len = key_set.shape[0]
    head_dim = queries.shape[1] // head_count
    scaling = head_dim ** -0.5
    q_heads = queries.astype(jnp.float32).reshape(seg_rows, head_count, head_dim)
    k_heads = key_set.astype(jnp.float32).reshape(key_len, head_count, head_dim)
    v_heads = value_set.astype(jnp.float32).reshape(key_len, head_count, head_dim)
    g_heads = grad_out.astype(jnp.float32).reshape(seg_rows, head_count, head_dim)
    scores = jnp.einsum("qhd,khd->hqk", q_heads, k_heads) * scaling
    scores = jnp.where(allowed[None], scores, -1e30)
    row_max = jnp.max(scores, axis=-1, keepdims=True)
    weights = jnp.where(allowed[None], jnp.exp(scores - row_max), 0.0)
    prob = weights / jnp.sum(weights, axis=-1, keepdims=True)
    prob_b = lax.optimization_barrier(prob.astype(jnp.bfloat16)).astype(jnp.float32)
    output = jnp.einsum("hqk,khd->qhd", prob_b, v_heads)
    output_b = lax.optimization_barrier(output.astype(jnp.bfloat16))
    output_f = output_b.astype(jnp.float32)
    dprob = jnp.einsum("qhd,khd->hqk", g_heads, v_heads)
    delta = jnp.sum(g_heads * output_f, axis=-1)
    dscore = prob * (dprob - jnp.transpose(delta)[:, :, None]) * scaling
    dscore_b = lax.optimization_barrier(dscore.astype(jnp.bfloat16)).astype(jnp.float32)
    grad_q = jnp.einsum("hqk,khd->qhd", dscore_b, k_heads).astype(jnp.bfloat16)
    grad_k = jnp.einsum("hqk,qhd->khd", dscore_b, q_heads)
    grad_v = jnp.einsum("hqk,qhd->khd", prob_b, g_heads)
    return (output_b.reshape(seg_rows, -1), grad_q.reshape(seg_rows, -1),
            grad_k.reshape(key_len, -1), grad_v.reshape(key_len, -1))


def reference(queries, keys, values, grad_out, cache, w_kv, doc_ids, routes):
    capacity = 2 * CACHE_DEV // N_SEQ
    slot_count = capacity * N_SEQ
    window = (SPAN + 1) * S
    pad_rows = SPAN * S
    features = H * HD

    def project(block):
        proj_k = jnp.dot(block.astype(jnp.float32), w_kv[0].astype(jnp.float32), preferred_element_type=jnp.float32)
        proj_v = jnp.dot(block.astype(jnp.float32), w_kv[1].astype(jnp.float32), preferred_element_type=jnp.float32)
        return jnp.stack([proj_k.astype(jnp.bfloat16), proj_v.astype(jnp.bfloat16)], 1)

    memory = lax.map(project, cache.reshape(N_SEQ, CACHE_DEV, CW)).reshape(N_SEQ * CACHE_DEV, 2, features)
    by_block = routes.reshape(N_SEQ, CACHE_DEV)
    targets = jnp.arange(N_SEQ, dtype=jnp.int32)
    onehot = (by_block[:, :, None] == targets[None, None, :]).astype(jnp.int32)
    ranks = jnp.sum((jnp.cumsum(onehot, axis=1) - onehot) * onehot, axis=2).astype(jnp.int32)
    sources = targets[:, None]
    place = (by_block * slot_count + sources * capacity + ranks).reshape(-1).astype(jnp.int32)
    table = jnp.zeros((N_SEQ * slot_count,), jnp.int32).at[place].set(jnp.arange(N_SEQ * CACHE_DEV, dtype=jnp.int32))
    filled = jnp.zeros((N_SEQ * slot_count,), jnp.bool_).at[place].set(True)
    key_pad = jnp.concatenate([jnp.zeros((pad_rows, features), keys.dtype), keys], 0)
    value_pad = jnp.concatenate([jnp.zeros((pad_rows, features), values.dtype), values], 0)
    id_pad = jnp.concatenate([jnp.full((pad_rows,), -1, jnp.int32), doc_ids.astype(jnp.int32)])

    def one_segment(accum, device):
        picked = lax.dynamic_slice_in_dim(table, device * slot_count, slot_count)
        live = lax.dynamic_slice_in_dim(filled, device * slot_count, slot_count)
        mem_rows = memory[picked]
        start = (device * S).astype(jnp.int32)
        seg_q = lax.dynamic_slice_in_dim(queries, start, S)
        seg_g = lax.dynamic_slice_in_dim(grad_out, start, S)
        win_k = lax.dynamic_slice_in_dim(key_pad, start, window)
        win_v = lax.dynamic_slice_in_dim(value_pad, start, window)
        q_ids = lax.dynamic_slice_in_dim(doc_ids.astype(jnp.int32), start, S)
        k_ids = lax.dynamic_slice_in_dim(id_pad, start, window)
        q_pos = start + jnp.arange(S, dtype=jnp.int32)
        k_pos = start - pad_rows + jnp.arange(window, dtype=jnp.int32)
        allowed_win = (k_pos[None, :] <= q_pos[:, None]) & (k_ids[None, :] == q_ids[:, None])
        allowed = jnp.concatenate([jnp.broadcast_to(live[None, :], (S, slot_count)), allowed_win], 1)
        key_set = jnp.concatenate([mem_rows[:, 0], win_k], 0)
        value_set = jnp.concatenate([mem_rows[:, 1], win_v], 0)
        output, grad_q, grad_k, grad_v = attend(seg_q, key_set, value_set, seg_g, allowed, H)
        update = jnp.stack([grad_k[slot_count:], grad_v[slot_count:]], 1)
        current = lax.dynamic_slice_in_dim(accum, start, window)
        accum = lax.dynamic_update_slice_in_dim(accum, current + update, start, 0)
        return accum, (output, grad_q)

    accum_start = jnp.zeros((pad_rows + TOKENS, 2, features), jnp.float32)
    accum, (outputs, grads) = lax.scan(one_segment, accum_start, jnp.arange(N_SEQ, dtype=jnp.int32))
    grad_kv = accum[pad_rows:]
    return (outputs.reshape(TOKENS, features), grads.reshape(TOKENS, features),
            grad_kv[:, 0].astype(jnp.bfloat16), grad_kv[:, 1].astype(jnp.bfloat16))
```

```python
import jax
import jax.numpy as jnp
from jax import lax
from jax.experimental import pallas as pl
from jax.experimental.pallas import tpu as pltpu
from jax.sharding import PartitionSpec as P

MESH = pl.DeviceIdType.MESH
NY, NX, NZ = 2, 4, 8
HD = 128
S = 128
HALF = 640
GROUPS = 5
FEAT = 1280
SLOTS = 256
NEG = -1e30
KINDS = "XZXZX"
POOL = 300


def near(offset):
    offset = offset % NZ
    return offset - NZ if offset > NZ // 2 else offset


def near_x(offset):
    offset = offset % NX
    return offset - NX if offset > NX // 2 else offset


def kernel(
    q_ref, k_ref, v_ref, g_ref, cache_ref, w_ref, doc_ref, route_ref,
    out_ref,
    rx0, wb, s_a, r_a, s_b, xb, kwb, vwb, qb, gb, bias, mem, gtx, grx, gown, stg,
    ssem, rsem, lsem,
):
    f32, bf16 = jnp.float32, jnp.bfloat16
    s = lax.axis_index("seq")
    h = lax.axis_index("head")
    c = lax.rem(s, 2)
    chip = s // 2
    z = lax.rem(chip, NZ)
    x = lax.rem(chip // NZ, NX)
    yh = chip // (NZ * NX)
    zp = lax.rem(z, 2)
    m = z // 2

    def dev(yy, xx, zz, cc, hh=None):
        return (((yy * NX + xx) * NZ + zz) * 2 + cc, h if hh is None else hh)

    def wrap(value, n):
        return lax.rem(value + 2 * n, n)

    sibling = dev(yh, x, z, 1 - c)
    other_head = (s, 1 - h)
    chips = NY * NX * NZ
    next_chip = lax.rem(chip + 1, chips)
    prev_chip = lax.rem(chip + chips - 1, chips)
    up = {"z+": dev(yh, x, wrap(z + 1, NZ), c), "z-": dev(yh, x, wrap(z - 1, NZ), c),
          "x+": dev(yh, wrap(x + 1, NX), z, c), "x-": dev(yh, wrap(x - 1, NX), z, c)}

    ids = {}
    sends = []

    def number(key):
        return ids.setdefault(key, len(ids))

    def send(key, src, dst, target):
        n = number(key)
        copy = pltpu.make_async_remote_copy(
            src_ref=src, dst_ref=dst, send_sem=ssem.at[n], recv_sem=rsem.at[n],
            device_id=target, device_id_type=MESH)
        copy.start()
        sends.append(copy)

    def recv(key, dst):
        n = number(key)
        pltpu.make_async_remote_copy(
            src_ref=dst, dst_ref=dst, send_sem=ssem.at[n], recv_sem=rsem.at[n],
            device_id=sibling, device_id_type=MESH).wait_recv()

    locals_ = []

    def local(src, dst):
        copy = pltpu.make_async_copy(src, dst, lsem.at[len(locals_)])
        copy.start()
        locals_.append(copy)
        return copy

    flips = [(a, b, d) for a in (0, 1) for b in (0, 1) for d in (0, 1) if a or b or d]
    rests = [(a, b, d) for a in (0, 1) for b in range(NX) for d in (0, 1) if a or b or d]

    barrier = pltpu.get_barrier_semaphore()
    greeted = [dev(wrap(yh + a, 2), x, 2 * m + wrap(zp + b, 2), wrap(c + d, 2)) for a, b, d in flips]
    greeted += [dev(yh, x, wrap(z + d, NZ), c) for d in range(1, NZ)]
    greeted += [dev(wrap(yh + a, 2), wrap(x + b, NX), z, wrap(c + d, 2)) for a, b, d in rests]
    greeted += [other_head]
    greeted += [(prev_chip * 2 + c, h), (prev_chip * 2 + 1 - c, h), (next_chip * 2 + c, h), (next_chip * 2 + 1 - c, h)]
    for target in greeted:
        pl.semaphore_signal(barrier, inc=1, device_id=target, device_id_type=MESH)
    pl.semaphore_wait(barrier, len(greeted))

    def cols(core):
        return pl.ds(pl.multiple_of(core * HALF, HD), HALF)

    def seg(index):
        return pl.ds(pl.multiple_of(index * S, S), S)

    mine = yh * 4 + zp * 2 + c
    for a, b, d in flips:
        zt, ct = wrap(zp + b, 2), wrap(c + d, 2)
        send(("p", a, b, d), w_ref.at[zt, :, cols(ct)], rx0.at[mine],
             dev(wrap(yh + a, 2), x, 2 * m + zt, ct))
    own_w = local(w_ref.at[zp, :, cols(c)], rx0.at[mine])

    route_own = route_ref[pl.ds(s, 1), :].astype(f32)
    row_i = lax.broadcasted_iota(jnp.int32, (S, S), 0)
    col_i = lax.broadcasted_iota(jnp.int32, (S, S), 1)
    route_col = jnp.sum(jnp.where(row_i == col_i, route_own, 0.0), axis=1, keepdims=True)
    same = (route_col == route_own) & (row_i < col_i)
    rank = jnp.sum(jnp.where(same, 1.0, 0.0), axis=0, keepdims=True)
    slot = lax.broadcasted_iota(jnp.int32, (SLOTS, S), 0)
    slot_z, slot_rest = slot // 32, lax.rem(slot // 2, 16)
    slot_dest = ((slot_rest // 2) * NZ + slot_z) * 2 + lax.rem(slot_rest, 2)
    chosen = (route_own == slot_dest.astype(f32)) & (rank == lax.rem(slot, 2).astype(f32))
    pick = jnp.where(chosen, 1.0, 0.0).astype(bf16)
    packed = jnp.dot(pick, cache_ref[...], preferred_element_type=f32).astype(bf16)
    s_a[...] = packed.reshape(NZ, 32, FEAT)
    for d in (4, 3, 5, 2, 6, 1, 7):
        zt = wrap(z + d, NZ)
        send(("a", d), s_a.at[zt], r_a.at[z], dev(yh, x, zt, c))
    own_a = local(s_a.at[z], r_a.at[z])

    def piece(g, xo, dz, part=None):
        zz = wrap(z + dz, NZ)
        xx = wrap(x + xo, NX)
        kv, mm = lax.rem(zz, 2), zz // 2
        if part is None:
            return wb.at[g, kv, :, xx, mm]
        return wb.at[g, kv, part, xx, mm]

    def pass_on(g, way, xo, dz, part=None):
        there_x = near_x(xo - {"x+": 1, "x-": -1}.get(way, 0))
        there_z = near(dz - {"z+": 1, "z-": -1}.get(way, 0))
        there = piece(g, xo, dz, part)
        send(("w", g, there_x, there_z, part), there, there, up[way])

    def got(g, xo, dz, part=None):
        recv(("w", g, xo, dz, part), piece(g, xo, dz, part))

    own_w.wait()
    for a, b, d in flips:
        source = wrap(yh + a, 2) * 4 + wrap(zp + b, 2) * 2 + wrap(c + d, 2)
        recv(("p", a, b, d), rx0.at[source])
    for y in range(2):
        block = jnp.concatenate([rx0[y * 4 + i].astype(f32) for i in range(4)], axis=0).astype(bf16)
        for g in range(GROUPS):
            wb[g, zp, y, x, m] = block[:, g * HD : (g + 1) * HD]

    for g in range(GROUPS):
        for way in ("x+", "x-", "z+", "z-"):
            pass_on(g, way, 0, 0)

    for name, ref, buf, segs in (("k", k_ref, kwb, True), ("v", v_ref, vwb, True), ("q", q_ref, qb, False), ("g", g_ref, gb, False)):
        base = 2 if segs else 0
        send((name, "s"), ref.at[:, cols(1 - c)], buf.at[seg(base + c)], sibling)
        local(ref.at[:, cols(c)], buf.at[seg(base + c)])
        if segs:
            for d in (0, 1):
                ct = wrap(c + d, 2)
                send((name, d), ref.at[:, cols(ct)], buf.at[seg(c)], (next_chip * 2 + ct, h))
    own_kv = list(locals_[2:])

    x_chunks = [g for g in range(GROUPS) if KINDS[g] == "X"]
    z_chunks = [g for g in range(GROUPS) if KINDS[g] == "Z"]

    def x_first(g, d):
        for sign, ahead in ((-1, "z+"), (1, "z-")):
            got(g, 0, sign * d)
            if d < 3:
                pass_on(g, ahead, 0, sign * d)
            else:
                pass_on(g, ahead, 0, sign * d, 0 if sign < 0 else 1)
            pass_on(g, "x+", 0, sign * d)
            pass_on(g, "x-", 0, sign * d)

    def x_first_last(g):
        got(g, 0, 4, 0)
        got(g, 0, 4, 1)
        pass_on(g, "x+", 0, 4)
        pass_on(g, "x-", 0, 4)

    def z_first(g):
        for sign, ahead in ((-1, "x+"), (1, "x-")):
            got(g, sign, 0)
            pass_on(g, ahead, sign, 0, 0 if sign < 0 else 1)
            pass_on(g, "z+", sign, 0)
            pass_on(g, "z-", sign, 0)

    def z_first_last(g):
        got(g, 2, 0, 0)
        got(g, 2, 0, 1)
        pass_on(g, "z+", 2, 0)
        pass_on(g, "z-", 2, 0)

    order = (0, -1, 1, -2, 2, -3, 3, 4)

    def x_last(g, lo, hi):
        for i in range(lo, hi):
            dz = order[i]
            got(g, -1, dz)
            if i % 2 == 0:
                pass_on(g, "x+", -1, dz)
            got(g, 1, dz)
            if i % 2 == 1:
                pass_on(g, "x-", 1, dz)

    def x_end(g):
        for dz in order:
            got(g, 2, dz)

    def z_last(g, d):
        for xo in (0, -1, 1, 2):
            for sign, ahead in ((-1, "z+"), (1, "z-")):
                got(g, xo, sign * d)
                if d < 3 or (xo in (0, -1)) == (sign < 0):
                    pass_on(g, ahead, xo, sign * d)

    def z_end(g):
        for xo in (0, -1, 1, 2):
            got(g, xo, 4)

    for g in range(GROUPS):
        if KINDS[g] == "X":
            x_first(g, 1)
        else:
            z_first(g)

    own_a.wait()
    for d in (4, 3, 5, 2, 6, 1, 7):
        recv(("a", d), r_a.at[wrap(z - d, NZ)])
    new_i = lax.broadcasted_iota(jnp.int32, (SLOTS, SLOTS), 0)
    old_i = lax.broadcasted_iota(jnp.int32, (SLOTS, SLOTS), 1)
    wanted = lax.rem(new_i // 2, NZ) * 32 + (new_i // 16) * 2 + lax.rem(new_i, 2)
    turn = jnp.where(old_i == wanted, 1.0, 0.0).astype(bf16)
    turned = jnp.dot(turn, r_a[...].reshape(SLOTS, FEAT), preferred_element_type=f32).astype(bf16)
    s_b[...] = turned.reshape(16, 16, FEAT)
    rest = (yh * NX + x) * 2 + c

    def x_rows(core, index):
        return pl.ds(pl.multiple_of(core * SLOTS + index * 16, 16), 16)

    for a, b, d in rests:
        yt, xt, ct = wrap(yh + a, 2), wrap(x + b, NX), wrap(c + d, 2)
        send(("b", a, b, d), s_b.at[(yt * NX + xt) * 2 + ct], xb.at[h, x_rows(ct, rest)], dev(yt, xt, z, ct))
    own_b = local(s_b.at[rest], xb.at[h, x_rows(c, rest)])

    for d in (2, 3):
        for g in x_chunks:
            x_first(g, d)
        if d == 2:
            for g in z_chunks:
                z_first_last(g)
    for g in x_chunks:
        x_first_last(g)

    diag = row_i == col_i
    dest_iota = lax.broadcasted_iota(jnp.int32, (S, SLOTS), 0)
    slot_iota = lax.broadcasted_iota(jnp.int32, (S, SLOTS), 1)
    slot_src = ((slot_iota // 32) * NZ + lax.rem(slot_iota // 2, NZ)) * 2 + lax.rem(slot_iota // 16, 2)
    spread = jnp.where(dest_iota == slot_src, 1.0, 0.0).astype(bf16)
    ones = jnp.ones((8, S), bf16)
    slot_no = lax.rem(lax.broadcasted_iota(jnp.int32, (1, SLOTS), 1), 2).astype(f32)
    for b in range(2):
        named = jnp.where(route_ref[...] == chip * 2 + b, 1.0, 0.0).astype(bf16)
        counts = lax.dot_general(ones, named, (((1,), (1,)), ((), ())), preferred_element_type=f32)
        by_slot = jnp.dot(counts.astype(bf16), spread, preferred_element_type=f32)[0:1]
        bias[b, :, 0:SLOTS] = jnp.broadcast_to(jnp.where(by_slot > slot_no, 0.0, NEG), (S, SLOTS))
        q_ids = doc_ref[pl.ds(chip * 2 + b, 1), :].astype(f32)
        q_col = jnp.sum(jnp.where(diag, q_ids, 0.0), axis=1, keepdims=True)
        for j in range(3):
            index = chip * 2 + b - 2 + j
            k_ids = doc_ref[pl.ds(jnp.maximum(index, 0), 1), :].astype(f32)
            k_ids = jnp.where(index >= 0, k_ids, -1.0)
            fits = q_col == k_ids
            if j == 2:
                fits = fits & (col_i <= row_i)
            bias[b, :, SLOTS + j * S : SLOTS + (j + 1) * S] = jnp.where(fits, 0.0, NEG)

    own_b.wait()
    for a, b, d in rests:
        recv(("b", a, b, d), xb.at[h, x_rows(c, (wrap(yh + a, 2) * NX + wrap(x - b, NX)) * 2 + wrap(c + d, 2))])

    def part_rows(core, i):
        return pl.ds(pl.multiple_of(core * SLOTS + i * 64, 64), 64)

    for i in range(4):
        here = xb.at[h, part_rows(c, i)]
        send(("h", i), here, here, other_head)
    for i in range(4):
        here = xb.at[h, part_rows(c, i)]
        send(("s", i), here, here, sibling)

    x_last(0, 0, 8)
    z_last(1, 1)
    z_last(1, 2)
    for i in range(4):
        here = xb.at[1 - h, part_rows(c, i)]
        recv(("h", i), here)
        send(("t", i), here, here, sibling)
    x_end(0)
    z_last(1, 3)
    x_last(2, 0, 8)
    z_end(1)
    for i in range(4):
        recv(("s", i), xb.at[h, part_rows(1 - c, i)])
        recv(("t", i), xb.at[1 - h, part_rows(1 - c, i)])
    for copy in own_kv:
        copy.wait()
    recv(("k", "s"), kwb.at[seg(3 - c)])
    recv(("v", "s"), vwb.at[seg(3 - c)])
    recv(("q", "s"), qb.at[seg(1 - c)])
    recv(("g", "s"), gb.at[seg(1 - c)])
    for d in (0, 1):
        recv(("k", d), kwb.at[seg(wrap(c + d, 2))])
        recv(("v", d), vwb.at[seg(wrap(c + d, 2))])

    nt = (((1,), (1,)), ((), ()))
    tn = (((0,), (0,)), ((), ()))
    scaling = HD ** -0.5

    def project(g):
        total = None
        for y in range(2):
            both = jnp.concatenate(
                [wb[g, kv, y].reshape(FEAT, HD) for kv in range(2)], axis=1)
            term = jnp.dot(xb[y], both, preferred_element_type=f32)
            total = term if total is None else total + term
        mem[0] = total[:, :HD].astype(bf16)
        mem[1] = total[:, HD:].astype(bf16)

    def attend(g):
        lanes = slice(g * HD, (g + 1) * HD)
        for b in range(2):
            rows = slice(b * S, (b + 1) * S)
            window = slice(b * S, b * S + 3 * S)
            query, cot = qb[rows, lanes], gb[rows, lanes]
            keys = jnp.concatenate([mem[0, b * SLOTS : (b + 1) * SLOTS], kwb[window, lanes]], axis=0)
            vals = jnp.concatenate([mem[1, b * SLOTS : (b + 1) * SLOTS], vwb[window, lanes]], axis=0)
            scores = lax.dot_general(query, keys, nt, preferred_element_type=f32) * scaling + bias[b]
            top = jnp.max(scores, axis=1, keepdims=True)
            weights = jnp.exp(scores - top)
            prob = weights * (1.0 / jnp.sum(weights, axis=1, keepdims=True))
            prob_b = prob.astype(bf16)
            out = jnp.dot(prob_b, vals, preferred_element_type=f32).astype(bf16)
            dprob = lax.dot_general(cot, vals, nt, preferred_element_type=f32)
            delta = jnp.sum(cot.astype(f32) * out.astype(f32), axis=1, keepdims=True)
            dscore = (prob * (dprob - delta) * scaling).astype(bf16)
            grad_q = jnp.dot(dscore, keys, preferred_element_type=f32).astype(bf16)
            stg[0, b, :, lanes] = out
            stg[1, b, :, lanes] = grad_q
            grad_k = lax.dot_general(dscore[:, SLOTS:], query, tn, preferred_element_type=f32)
            grad_v = lax.dot_general(prob_b[:, SLOTS:], cot, tn, preferred_element_type=f32)
            for i, grad in enumerate((grad_k, grad_v)):
                if b == 0:
                    gown[g, i, 0 : 3 * S] = grad
                else:
                    gown[g, i, S : 3 * S] += grad[: 2 * S]
                    gown[g, i, 3 * S :] = grad[2 * S :]
        for i in range(2):
            gtx[g, i] = gown[g, i, : 2 * S].astype(bf16)
        send(("e", g), gtx.at[g], grx.at[g], (prev_chip * 2 + c, h))
        hand_over(g, 0)

    def hand_over(g, first):
        lanes = pl.ds(g * HD, HD)
        there = out_ref.at[pl.ds(first, 2), :, pl.ds(pl.multiple_of(c * HALF + g * HD, HD), HD)]
        send(("o", g, first), stg.at[pl.ds(first, 2), 1 - c, :, lanes], there, sibling)
        local(stg.at[pl.ds(first, 2), c, :, lanes], there)

    def finish(g):
        lanes = slice(g * HD, (g + 1) * HD)
        recv(("e", g), grx.at[g])
        for i in range(2):
            total = (gown[g, i, 2 * S :] + grx[g, i].astype(f32)).astype(bf16)
            for b in range(2):
                stg[2 + i, b, :, lanes] = total[b * S : (b + 1) * S]
        hand_over(g, 2)

    project(0)
    z_last(3, 1)
    x_last(4, 0, 4)
    attend(0)
    z_last(3, 2)
    x_last(4, 4, 8)
    project(1)
    x_end(2)
    z_last(3, 3)
    attend(1)
    project(2)
    attend(2)
    finish(0)
    z_end(3)
    project(3)
    attend(3)
    finish(1)
    finish(2)
    x_end(4)
    project(4)
    attend(4)
    finish(3)
    finish(4)
    for g in range(GROUPS):
        for first in (0, 2):
            recv(("o", g, first), out_ref.at[
                pl.ds(first, 2), :, pl.ds(pl.multiple_of((1 - c) * HALF + g * HD, HD), HD)])
    for copy in locals_[len(own_kv) + 3 :]:
        copy.wait()
    for copy in sends:
        copy.wait_send()
    assert len(ids) <= POOL


def body(queries, keys, values, grad_out, cache, w_kv, doc_ids, routes):
    bf16, f32 = jnp.bfloat16, jnp.float32
    vmem = pl.BlockSpec(memory_space=pltpu.VMEM)
    result = pl.pallas_call(
        kernel,
        out_shape=jax.ShapeDtypeStruct((4, S, FEAT), bf16),
        in_specs=[vmem] * 8,
        out_specs=vmem,
        scratch_shapes=[
            pltpu.VMEM((8, 20, HALF), bf16),
            pltpu.VMEM((GROUPS, 2, NY, NX, NZ // 2, 80, HD), bf16),
            pltpu.VMEM((NZ, 32, FEAT), bf16),
            pltpu.VMEM((NZ, 32, FEAT), bf16),
            pltpu.VMEM((16, 16, FEAT), bf16),
            pltpu.VMEM((2, 2 * SLOTS, FEAT), bf16),
            pltpu.VMEM((4 * S, HALF), bf16),
            pltpu.VMEM((4 * S, HALF), bf16),
            pltpu.VMEM((2 * S, HALF), bf16),
            pltpu.VMEM((2 * S, HALF), bf16),
            pltpu.VMEM((2, S, SLOTS + 3 * S), f32),
            pltpu.VMEM((2, 2 * SLOTS, HD), bf16),
            pltpu.VMEM((GROUPS, 2, 2 * S, HD), bf16),
            pltpu.VMEM((GROUPS, 2, 2 * S, HD), bf16),
            pltpu.VMEM((GROUPS, 2, 4 * S, HD), f32),
            pltpu.VMEM((4, 2, S, HALF), bf16),
            pltpu.SemaphoreType.DMA((POOL,)),
            pltpu.SemaphoreType.DMA((POOL,)),
            pltpu.SemaphoreType.DMA((24,)),
        ],
        compiler_params=pltpu.CompilerParams(
            collective_id=0, has_side_effects=True, vmem_limit_bytes=50 * 2**20
        ),
        name="segment_layer",
    )(queries, keys, values, grad_out, cache, w_kv, doc_ids.reshape(S, S), routes.reshape(S, S))
    return (result[0], result[1], result[2], result[3])


def solution(mesh):
    rows = P("seq", "head")
    return jax.shard_map(
        body,
        mesh=mesh,
        in_specs=(rows, rows, rows, rows, rows, P(None, "seq", "head"), P(), P()),
        out_specs=(rows, rows, rows, rows),
        check_vma=False,
    )
```

```python
import jax
import jax.numpy as jnp
from jax import lax
from jax.experimental import pallas as pl
from jax.experimental.pallas import tpu as pltpu
from jax.sharding import PartitionSpec as P

MESH = pl.DeviceIdType.MESH
NY, NX, NZ = 2, 4, 8
HD = 128
S = 128
HALF = 640
GROUPS = 5
FEAT = 1280
SLOTS = 256
NEG = -1e30
KINDS = "XZXXX"
CHUNKS = ((0, 512), (512, 512), (1024, 256))
POOL = 340


def near(offset):
    offset = offset % NZ
    return offset - NZ if offset > NZ // 2 else offset


def near_x(offset):
    offset = offset % NX
    return offset - NX if offset > NX // 2 else offset


def kernel(
    q_ref, k_ref, v_ref, g_ref, cache_ref, w_ref, doc_ref, route_ref,
    out_ref,
    routes, docs, held, rx0, wb, s_b, r_b, s_a, xb, kwb, vwb, qb, gb, bias, mem, gtx, grx, gown, stg,
    ssem, rsem, lsem,
):
    f32, bf16 = jnp.float32, jnp.bfloat16
    s = lax.axis_index("seq")
    h = lax.axis_index("head")
    c = lax.rem(s, 2)
    chip = s // 2
    z = lax.rem(chip, NZ)
    x = lax.rem(chip // NZ, NX)
    yh = chip // (NZ * NX)
    zp = lax.rem(z, 2)
    m = z // 2

    def dev(yy, xx, zz, cc, hh=None):
        return (((yy * NX + xx) * NZ + zz) * 2 + cc, h if hh is None else hh)

    def wrap(value, n):
        return lax.rem(value + 2 * n, n)

    sibling = dev(yh, x, z, 1 - c)
    other_head = (s, 1 - h)
    chips = NY * NX * NZ
    next_chip = lax.rem(chip + 1, chips)
    prev_chip = lax.rem(chip + chips - 1, chips)
    up = {"z+": dev(yh, x, wrap(z + 1, NZ), c), "z-": dev(yh, x, wrap(z - 1, NZ), c),
          "x+": dev(yh, wrap(x + 1, NX), z, c), "x-": dev(yh, wrap(x - 1, NX), z, c)}

    ids = {}
    sends = []

    def number(key):
        return ids.setdefault(key, len(ids))

    def send(key, src, dst, target):
        n = number(key)
        copy = pltpu.make_async_remote_copy(
            src_ref=src, dst_ref=dst, send_sem=ssem.at[n], recv_sem=rsem.at[n],
            device_id=target, device_id_type=MESH)
        copy.start()
        sends.append(copy)

    def recv(key, dst):
        n = number(key)
        pltpu.make_async_remote_copy(
            src_ref=dst, dst_ref=dst, send_sem=ssem.at[n], recv_sem=rsem.at[n],
            device_id=sibling, device_id_type=MESH).wait_recv()

    locals_ = []

    def local(src, dst):
        copy = pltpu.make_async_copy(src, dst, lsem.at[len(locals_)])
        copy.start()
        locals_.append(copy)
        return copy

    flips = [(a, b, d) for a in (0, 1) for b in (0, 1) for d in (0, 1) if a or b or d]
    planes = [(a, b) for a, b in ((1, 2), (0, 2), (1, 1), (1, 3), (1, 0), (0, 1), (0, 3))]

    route_load = local(route_ref, routes)
    doc_load = local(doc_ref, docs)
    held_load = local(cache_ref, held)

    barrier = pltpu.get_barrier_semaphore()
    greeted = [dev(wrap(yh + a, 2), x, 2 * m + wrap(zp + b, 2), wrap(c + d, 2)) for a, b, d in flips]
    greeted += [dev(yh, x, wrap(z + d, NZ), c) for d in range(1, NZ)]
    greeted += [dev(wrap(yh + a, 2), wrap(x + b, NX), z, c) for a, b in planes]
    greeted += [other_head]
    greeted += [(prev_chip * 2 + c, h), (prev_chip * 2 + 1 - c, h), (next_chip * 2 + c, h), (next_chip * 2 + 1 - c, h)]
    for target in greeted:
        pl.semaphore_signal(barrier, inc=1, device_id=target, device_id_type=MESH)

    def cols(core):
        return pl.ds(pl.multiple_of(core * HALF, HD), HALF)

    def seg(index):
        return pl.ds(pl.multiple_of(index * S, S), S)

    route_load.wait()
    route_own = routes[pl.ds(s, 1), :].astype(f32)
    row_i = lax.broadcasted_iota(jnp.int32, (S, S), 0)
    col_i = lax.broadcasted_iota(jnp.int32, (S, S), 1)
    route_col = jnp.sum(jnp.where(row_i == col_i, route_own, 0.0), axis=1, keepdims=True)
    same = (route_col == route_own) & (row_i < col_i)
    rank = jnp.sum(jnp.where(same, 1.0, 0.0), axis=0, keepdims=True)
    slot = lax.broadcasted_iota(jnp.int32, (SLOTS, S), 0)
    chosen = (route_own == (slot // 2).astype(f32)) & (rank == lax.rem(slot, 2).astype(f32))
    pick = jnp.where(chosen, 1.0, 0.0).astype(bf16)

    pl.semaphore_wait(barrier, len(greeted))

    mine = yh * 4 + zp * 2 + c
    for a, b, d in flips:
        zt, ct = wrap(zp + b, 2), wrap(c + d, 2)
        send(("p", a, b, d), w_ref.at[zt, :, cols(ct)], rx0.at[mine],
             dev(wrap(yh + a, 2), x, 2 * m + zt, ct))
    own_w = local(w_ref.at[zp, :, cols(c)], rx0.at[mine])

    held_load.wait()
    plane = yh * NX + x
    own_b = []
    for i, (first, count) in enumerate(CHUNKS):
        lanes = slice(first, first + count)
        packed = jnp.dot(pick, held[:, lanes], preferred_element_type=f32).astype(bf16)
        s_b[:, :, lanes] = packed.reshape(NY * NX, 32, count)
        lanes = pl.ds(first, count)
        for a, b in planes:
            yt, xt = wrap(yh + a, 2), wrap(x + b, NX)
            send(("b", i, a, b), s_b.at[yt * NX + xt, :, lanes], r_b.at[plane, :, lanes], dev(yt, xt, z, c))
        own_b.append(local(s_b.at[plane, :, lanes], r_b.at[plane, :, lanes]))

    def piece(g, xo, dz, part=None):
        zz = wrap(z + dz, NZ)
        xx = wrap(x + xo, NX)
        kv, mm = lax.rem(zz, 2), zz // 2
        if KINDS[g] in "PQ":
            return wb.at[g, kv, yh, xx, mm]
        if part is None:
            return wb.at[g, kv, :, xx, mm]
        return wb.at[g, kv, part, xx, mm]

    def pass_on(g, way, xo, dz, part=None):
        there_x = near_x(xo - {"x+": 1, "x-": -1}.get(way, 0))
        there_z = near(dz - {"z+": 1, "z-": -1}.get(way, 0))
        there = piece(g, xo, dz, part)
        send(("w", g, there_x, there_z, part), there, there, up[way])

    def got(g, xo, dz, part=None):
        recv(("w", g, xo, dz, part), piece(g, xo, dz, part))
        if KINDS[g] in "PQ":
            cross(g, xo, dz)

    def cross(g, xo, dz):
        there = piece(g, xo, dz)
        send(("y", g, xo, dz), there, there, dev(1 - yh, x, z, c))

    def crossed(g, xo, dz):
        zz = wrap(z + dz, NZ)
        recv(("y", g, xo, dz), wb.at[g, lax.rem(zz, 2), 1 - yh, wrap(x + xo, NX), zz // 2])

    def crossed_all(g):
        if KINDS[g] not in "PQ":
            return
        for xo in (0, -1, 1, 2):
            for dz in order:
                crossed(g, xo, dz)

    own_w.wait()
    for a, b, d in flips:
        source = wrap(yh + a, 2) * 4 + wrap(zp + b, 2) * 2 + wrap(c + d, 2)
        recv(("p", a, b, d), rx0.at[source])
    for y in range(2):
        block = jnp.concatenate([rx0[y * 4 + i].astype(f32) for i in range(4)], axis=0).astype(bf16)
        for g in range(GROUPS):
            wb[g, zp, y, x, m] = block[:, g * HD : (g + 1) * HD]

    for g in range(GROUPS):
        for way in ("x+", "x-", "z+", "z-"):
            pass_on(g, way, 0, 0)
        if KINDS[g] in "PQ":
            cross(g, 0, 0)

    order = (0, -1, 1, -2, 2, -3, 3, 4)

    def x_first(g, d):
        whole = KINDS[g] == "P"
        for sign, ahead in ((-1, "z+"), (1, "z-")):
            got(g, 0, sign * d)
            if d < 3:
                pass_on(g, ahead, 0, sign * d)
            elif not whole:
                pass_on(g, ahead, 0, sign * d, 0 if sign < 0 else 1)
            elif sign < 0:
                pass_on(g, ahead, 0, sign * d)
            pass_on(g, "x+", 0, sign * d)
            pass_on(g, "x-", 0, sign * d)

    def x_first_last(g):
        if KINDS[g] == "P":
            got(g, 0, 4)
        else:
            got(g, 0, 4, 0)
            got(g, 0, 4, 1)
        pass_on(g, "x+", 0, 4)
        pass_on(g, "x-", 0, 4)

    def z_first(g):
        for sign, ahead in ((-1, "x+"), (1, "x-")):
            got(g, sign, 0)
            if sign < 0:
                pass_on(g, ahead, sign, 0)
            pass_on(g, "z+", sign, 0)
            pass_on(g, "z-", sign, 0)

    def z_first_last(g):
        got(g, 2, 0)
        pass_on(g, "z+", 2, 0)
        pass_on(g, "z-", 2, 0)

    def x_last(g, lo, hi):
        for i in range(lo, hi):
            dz = order[i]
            got(g, -1, dz)
            if i % 2 == 0:
                pass_on(g, "x+", -1, dz)
            got(g, 1, dz)
            if i % 2 == 1:
                pass_on(g, "x-", 1, dz)

    def x_end(g):
        for dz in order:
            got(g, 2, dz)

    def z_last(g, d):
        for xo in (0, -1, 1, 2):
            for sign, ahead in ((-1, "z+"), (1, "z-")):
                got(g, xo, sign * d)
                if d < 3 or (xo in (0, -1)) == (sign < 0):
                    pass_on(g, ahead, xo, sign * d)

    def z_end(g):
        for xo in (0, -1, 1, 2):
            got(g, xo, 4)

    def last(g, stage):
        if KINDS[g] in "XP":
            if stage < 3:
                x_last(g, (0, 3, 6)[stage], (3, 6, 8)[stage])
            else:
                x_end(g)
        elif stage < 3:
            z_last(g, stage + 1)
        else:
            z_end(g)

    x_chunks = [g for g in range(GROUPS) if KINDS[g] in "XP"]
    z_chunks = [g for g in range(GROUPS) if KINDS[g] in "QZ"]
    for g in x_chunks:
        x_first(g, 1)
    for g in z_chunks:
        z_first(g)

    new_i = lax.broadcasted_iota(jnp.int32, (SLOTS, SLOTS), 0)
    old_i = lax.broadcasted_iota(jnp.int32, (SLOTS, SLOTS), 1)
    wanted = lax.rem(new_i // 2, 8) * 32 + (new_i // 16) * 2 + lax.rem(new_i, 2)
    turn = jnp.where(old_i == wanted, 1.0, 0.0).astype(bf16)
    own_a = []
    for i, (first, count) in enumerate(CHUNKS):
        lanes = slice(first, first + count)
        own_b[i].wait()
        for a, b in planes:
            recv(("b", i, a, b), r_b.at[wrap(yh + a, 2) * NX + wrap(x - b, NX), :, pl.ds(first, count)])
        old = r_b[:, :, lanes].reshape(SLOTS, count)
        s_a[:, :, lanes] = jnp.dot(turn, old, preferred_element_type=f32).astype(bf16).reshape(NZ, 32, count)
        lanes = pl.ds(first, count)
        for d in (4, 3, 5, 2, 6, 1, 7):
            zt = wrap(z + d, NZ)
            send(("a", i, d), s_a.at[zt, :, lanes], xb.at[h, c, z, :, lanes], dev(yh, x, zt, c))
        own_a.append(local(s_a.at[z, :, lanes], xb.at[h, c, z, :, lanes]))

    for g in x_chunks:
        x_first(g, 2)
    for g in z_chunks:
        z_first_last(g)

    for g in x_chunks:
        x_first(g, 3)
    for g in x_chunks:
        x_first_last(g)

    doc_load.wait()
    diag = row_i == col_i
    src_iota = lax.broadcasted_iota(jnp.int32, (S, SLOTS), 0)
    slot_iota = lax.broadcasted_iota(jnp.int32, (S, SLOTS), 1)
    slot_src = (lax.rem(slot_iota // 2, 8) * NZ + lax.rem(slot_iota // 16, NZ)) * 2 + slot_iota // S
    spread = jnp.where(src_iota == slot_src, 1.0, 0.0).astype(bf16)
    ones = jnp.ones((8, S), bf16)
    slot_no = lax.rem(lax.broadcasted_iota(jnp.int32, (1, SLOTS), 1), 2).astype(f32)
    for b in range(2):
        named = jnp.where(routes[...] == chip * 2 + b, 1.0, 0.0).astype(bf16)
        counts = lax.dot_general(ones, named, (((1,), (1,)), ((), ())), preferred_element_type=f32)
        by_slot = jnp.dot(counts.astype(bf16), spread, preferred_element_type=f32)[0:1]
        bias[b, :, 0:SLOTS] = jnp.broadcast_to(jnp.where(by_slot > slot_no, 0.0, NEG), (S, SLOTS))
        q_ids = docs[pl.ds(chip * 2 + b, 1), :].astype(f32)
        q_col = jnp.sum(jnp.where(diag, q_ids, 0.0), axis=1, keepdims=True)
        for j in range(3):
            index = chip * 2 + b - 2 + j
            k_ids = docs[pl.ds(jnp.maximum(index, 0), 1), :].astype(f32)
            k_ids = jnp.where(index >= 0, k_ids, -1.0)
            fits = q_col == k_ids
            if j == 2:
                fits = fits & (col_i <= row_i)
            bias[b, :, SLOTS + j * S : SLOTS + (j + 1) * S] = jnp.where(fits, 0.0, NEG)

    def spread_rows(i):
        lanes = pl.ds(*CHUNKS[i])
        own_a[i].wait()
        for d in (4, 3, 5, 2, 6, 1, 7):
            recv(("a", i, d), xb.at[h, c, wrap(z - d, NZ), :, lanes])
        here = xb.at[h, c, :, :, lanes]
        send(("h", i), here, here, other_head)
        send(("s", i), here, here, sibling)

    def forward_rows(i):
        here = xb.at[1 - h, c, :, :, pl.ds(*CHUNKS[i])]
        recv(("h", i), here)
        send(("t", i), here, here, sibling)

    last(0, 0)
    last(1, 0)
    spread_rows(0)
    own_kv = []
    for name, ref, buf, segs in (("k", k_ref, kwb, True), ("v", v_ref, vwb, True), ("q", q_ref, qb, False), ("g", g_ref, gb, False)):
        base = 2 if segs else 0
        send((name, "s"), ref.at[:, cols(1 - c)], buf.at[seg(base + c)], sibling)
        own_kv.append(local(ref.at[:, cols(c)], buf.at[seg(base + c)]))
        if segs:
            for d in (0, 1):
                ct = wrap(c + d, 2)
                send((name, d), ref.at[:, cols(ct)], buf.at[seg(c)], (next_chip * 2 + ct, h))

    last(0, 1)
    last(1, 1)
    spread_rows(1)
    last(0, 2)
    last(1, 2)
    spread_rows(2)
    forward_rows(0)
    last(0, 3)
    last(2, 0)
    forward_rows(1)
    last(1, 3)
    last(2, 1)
    last(3, 0)
    forward_rows(2)
    last(2, 2)
    last(3, 1)
    for i in range(len(CHUNKS)):
        lanes = pl.ds(*CHUNKS[i])
        recv(("s", i), xb.at[h, 1 - c, :, :, lanes])
        recv(("t", i), xb.at[1 - h, 1 - c, :, :, lanes])
    handed = []
    nt = (((1,), (1,)), ((), ()))
    tn = (((0,), (0,)), ((), ()))
    scaling = HD ** -0.5

    def project(g):
        total = None
        for y in range(2):
            both = jnp.concatenate(
                [wb[g, kv, y].reshape(FEAT, HD) for kv in range(2)], axis=1)
            term = jnp.dot(xb[y].reshape(2 * SLOTS, FEAT), both, preferred_element_type=f32)
            total = term if total is None else total + term
        mem[0] = total[:, :HD].astype(bf16).reshape(16, 2, 16, HD)
        mem[1] = total[:, HD:].astype(bf16).reshape(16, 2, 16, HD)

    def attend(g):
        lanes = slice(g * HD, (g + 1) * HD)
        for b in range(2):
            rows = slice(b * S, (b + 1) * S)
            window = slice(b * S, b * S + 3 * S)
            query, cot = qb[rows, lanes], gb[rows, lanes]
            keys = jnp.concatenate([mem[0, :, b].reshape(SLOTS, HD), kwb[window, lanes]], axis=0)
            vals = jnp.concatenate([mem[1, :, b].reshape(SLOTS, HD), vwb[window, lanes]], axis=0)
            scores = lax.dot_general(query, keys, nt, preferred_element_type=f32) * scaling + bias[b]
            top = jnp.max(scores, axis=1, keepdims=True)
            weights = jnp.exp(scores - top)
            prob = weights * (1.0 / jnp.sum(weights, axis=1, keepdims=True))
            prob_b = prob.astype(bf16)
            out = jnp.dot(prob_b, vals, preferred_element_type=f32).astype(bf16)
            dprob = lax.dot_general(cot, vals, nt, preferred_element_type=f32)
            delta = jnp.sum(cot.astype(f32) * out.astype(f32), axis=1, keepdims=True)
            dscore = (prob * (dprob - delta) * scaling).astype(bf16)
            grad_q = jnp.dot(dscore, keys, preferred_element_type=f32).astype(bf16)
            stg[0, b, :, lanes] = out
            stg[1, b, :, lanes] = grad_q
            grad_k = lax.dot_general(dscore[:, SLOTS:], query, tn, preferred_element_type=f32)
            grad_v = lax.dot_general(prob_b[:, SLOTS:], cot, tn, preferred_element_type=f32)
            for i, grad in enumerate((grad_k, grad_v)):
                if b == 0:
                    gown[g, i, 0 : 3 * S] = grad
                else:
                    gown[g, i, S : 3 * S] += grad[: 2 * S]
                    gown[g, i, 3 * S :] = grad[2 * S :]
        for i in range(2):
            gtx[g, i] = gown[g, i, : 2 * S].astype(bf16)
        send(("e", g), gtx.at[g], grx.at[g], (prev_chip * 2 + c, h))
        hand_over(g, 0)

    def hand_over(g, first):
        lanes = pl.ds(g * HD, HD)
        there = out_ref.at[pl.ds(first, 2), :, pl.ds(pl.multiple_of(c * HALF + g * HD, HD), HD)]
        send(("o", g, first), stg.at[pl.ds(first, 2), 1 - c, :, lanes], there, sibling)
        handed.append(local(stg.at[pl.ds(first, 2), c, :, lanes], there))

    def finish(g):
        lanes = slice(g * HD, (g + 1) * HD)
        recv(("e", g), grx.at[g])
        for i in range(2):
            total = (gown[g, i, 2 * S :] + grx[g, i].astype(f32)).astype(bf16)
            for b in range(2):
                stg[2 + i, b, :, lanes] = total[b * S : (b + 1) * S]
        hand_over(g, 2)

    crossed_all(0)
    project(0)
    last(4, 0)
    last(3, 2)
    for copy in own_kv:
        copy.wait()
    recv(("k", "s"), kwb.at[seg(3 - c)])
    recv(("v", "s"), vwb.at[seg(3 - c)])
    recv(("q", "s"), qb.at[seg(1 - c)])
    recv(("g", "s"), gb.at[seg(1 - c)])
    for d in (0, 1):
        recv(("k", d), kwb.at[seg(wrap(c + d, 2))])
        recv(("v", d), vwb.at[seg(wrap(c + d, 2))])

    attend(0)
    last(4, 1)
    last(2, 3)
    crossed_all(1)
    project(1)
    last(4, 2)
    attend(1)
    crossed_all(2)
    project(2)
    attend(2)
    finish(0)
    last(3, 3)
    crossed_all(3)
    project(3)
    attend(3)
    finish(1)
    finish(2)
    last(4, 3)
    crossed_all(4)
    project(4)
    attend(4)
    finish(3)
    finish(4)
    for g in range(GROUPS):
        for first in (0, 2):
            recv(("o", g, first), out_ref.at[
                pl.ds(first, 2), :, pl.ds(pl.multiple_of((1 - c) * HALF + g * HD, HD), HD)])
    for copy in handed:
        copy.wait()
    for copy in sends:
        copy.wait_send()
    assert len(ids) <= POOL


def body(queries, keys, values, grad_out, cache, w_kv, doc_ids, routes):
    bf16, f32 = jnp.bfloat16, jnp.float32
    vmem = pl.BlockSpec(memory_space=pltpu.VMEM)
    hbm = pl.BlockSpec(memory_space=pltpu.HBM)
    result = pl.pallas_call(
        kernel,
        out_shape=jax.ShapeDtypeStruct((4, S, FEAT), bf16),
        in_specs=[hbm] * 5 + [vmem] + [hbm] * 2,
        out_specs=vmem,
        scratch_shapes=[
            pltpu.VMEM((S, S), jnp.int32),
            pltpu.VMEM((S, S), jnp.int32),
            pltpu.VMEM((S, FEAT), bf16),
            pltpu.VMEM((8, 20, HALF), bf16),
            pltpu.VMEM((GROUPS, 2, NY, NX, NZ // 2, 80, HD), bf16),
            pltpu.VMEM((NZ, 32, FEAT), bf16),
            pltpu.VMEM((NZ, 32, FEAT), bf16),
            pltpu.VMEM((NZ, 32, FEAT), bf16),
            pltpu.VMEM((2, 2, NZ, 32, FEAT), bf16),
            pltpu.VMEM((4 * S, HALF), bf16),
            pltpu.VMEM((4 * S, HALF), bf16),
            pltpu.VMEM((2 * S, HALF), bf16),
            pltpu.VMEM((2 * S, HALF), bf16),
            pltpu.VMEM((2, S, SLOTS + 3 * S), f32),
            pltpu.VMEM((2, 16, 2, 16, HD), bf16),
            pltpu.VMEM((GROUPS, 2, 2 * S, HD), bf16),
            pltpu.VMEM((GROUPS, 2, 2 * S, HD), bf16),
            pltpu.VMEM((GROUPS, 2, 4 * S, HD), f32),
            pltpu.VMEM((4, 2, S, HALF), bf16),
            pltpu.SemaphoreType.DMA((POOL,)),
            pltpu.SemaphoreType.DMA((POOL,)),
            pltpu.SemaphoreType.DMA((32,)),
        ],
        compiler_params=pltpu.CompilerParams(
            collective_id=0, has_side_effects=True, vmem_limit_bytes=64 * 2**20
        ),
        name="segment_layer",
    )(queries, keys, values, grad_out, cache, w_kv, doc_ids.reshape(S, S), routes.reshape(S, S))
    return (result[0], result[1], result[2], result[3])


def solution(mesh):
    rows = P("seq", "head")
    return jax.shard_map(
        body,
        mesh=mesh,
        in_specs=(rows, rows, rows, rows, rows, P(None, "seq", "head"), P(), P()),
        out_specs=(rows, rows, rows, rows),
        check_vma=False,
    )
```

```python
import jax
import jax.numpy as jnp
from jax import lax
from jax.experimental import pallas as pl
from jax.experimental.pallas import tpu as pltpu
from jax.sharding import PartitionSpec as P

MESH = pl.DeviceIdType.MESH
NY, NX, NZ = 2, 4, 8
HD = 128
S = 128
HALF = 640
GROUPS = 5
FEAT = 1280
SLOTS = 256
NEG = -1e30
KINDS = "ZXXXX"
CHUNKS = ((0, 512), (512, 512), (1024, 256))
POOL = 340


def near(offset):
    offset = offset % NZ
    return offset - NZ if offset > NZ // 2 else offset


def near_x(offset):
    offset = offset % NX
    return offset - NX if offset > NX // 2 else offset


def kernel(
    q_ref, k_ref, v_ref, g_ref, cache_ref, w_ref, doc_ref, route_ref,
    out_ref,
    routes, docs, held, rx0, wb, s_b, r_b, s_a, xb, kwb, vwb, qb, gb, bias, mem, gtx, grx, gown, stg,
    ssem, rsem, lsem,
):
    f32, bf16 = jnp.float32, jnp.bfloat16
    s = lax.axis_index("seq")
    h = lax.axis_index("head")
    c = lax.rem(s, 2)
    chip = s // 2
    z = lax.rem(chip, NZ)
    x = lax.rem(chip // NZ, NX)
    yh = chip // (NZ * NX)
    zp = lax.rem(z, 2)
    m = z // 2

    def dev(yy, xx, zz, cc, hh=None):
        return (((yy * NX + xx) * NZ + zz) * 2 + cc, h if hh is None else hh)

    def wrap(value, n):
        return lax.rem(value + 2 * n, n)

    sibling = dev(yh, x, z, 1 - c)
    other_head = (s, 1 - h)
    chips = NY * NX * NZ
    next_chip = lax.rem(chip + 1, chips)
    prev_chip = lax.rem(chip + chips - 1, chips)
    up = {"z+": dev(yh, x, wrap(z + 1, NZ), c), "z-": dev(yh, x, wrap(z - 1, NZ), c),
          "x+": dev(yh, wrap(x + 1, NX), z, c), "x-": dev(yh, wrap(x - 1, NX), z, c)}

    ids = {}
    sends = []

    def number(key):
        return ids.setdefault(key, len(ids))

    def send(key, src, dst, target):
        n = number(key)
        copy = pltpu.make_async_remote_copy(
            src_ref=src, dst_ref=dst, send_sem=ssem.at[n], recv_sem=rsem.at[n],
            device_id=target, device_id_type=MESH)
        copy.start()
        sends.append(copy)

    def recv(key, dst):
        n = number(key)
        pltpu.make_async_remote_copy(
            src_ref=dst, dst_ref=dst, send_sem=ssem.at[n], recv_sem=rsem.at[n],
            device_id=sibling, device_id_type=MESH).wait_recv()

    locals_ = []

    def local(src, dst):
        copy = pltpu.make_async_copy(src, dst, lsem.at[len(locals_)])
        copy.start()
        locals_.append(copy)
        return copy

    flips = [(a, b, d) for a in (0, 1) for b in (0, 1) for d in (0, 1) if a or b or d]
    planes = [(a, b) for a, b in ((1, 2), (0, 2), (1, 1), (1, 3), (1, 0), (0, 1), (0, 3))]

    route_load = local(route_ref, routes)
    doc_load = local(doc_ref, docs)
    held_load = local(cache_ref, held)

    barrier = pltpu.get_barrier_semaphore()
    greeted = [dev(wrap(yh + a, 2), x, 2 * m + wrap(zp + b, 2), wrap(c + d, 2)) for a, b, d in flips]
    greeted += [dev(yh, x, wrap(z + d, NZ), c) for d in range(1, NZ)]
    greeted += [dev(wrap(yh + a, 2), wrap(x + b, NX), z, c) for a, b in planes]
    greeted += [other_head]
    greeted += [(prev_chip * 2 + c, h), (prev_chip * 2 + 1 - c, h), (next_chip * 2 + c, h), (next_chip * 2 + 1 - c, h)]
    for target in greeted:
        pl.semaphore_signal(barrier, inc=1, device_id=target, device_id_type=MESH)

    def cols(core):
        return pl.ds(pl.multiple_of(core * HALF, HD), HALF)

    def seg(index):
        return pl.ds(pl.multiple_of(index * S, S), S)

    route_load.wait()
    route_own = routes[pl.ds(s, 1), :].astype(f32)
    row_i = lax.broadcasted_iota(jnp.int32, (S, S), 0)
    col_i = lax.broadcasted_iota(jnp.int32, (S, S), 1)
    route_col = jnp.sum(jnp.where(row_i == col_i, route_own, 0.0), axis=1, keepdims=True)
    same = (route_col == route_own) & (row_i < col_i)
    rank = jnp.sum(jnp.where(same, 1.0, 0.0), axis=0, keepdims=True)
    slot = lax.broadcasted_iota(jnp.int32, (SLOTS, S), 0)
    chosen = (route_own == (slot // 2).astype(f32)) & (rank == lax.rem(slot, 2).astype(f32))
    pick = jnp.where(chosen, 1.0, 0.0).astype(bf16)

    pl.semaphore_wait(barrier, len(greeted))

    mine = yh * 4 + zp * 2 + c
    for a, b, d in flips:
        zt, ct = wrap(zp + b, 2), wrap(c + d, 2)
        send(("p", a, b, d), w_ref.at[zt, :, cols(ct)], rx0.at[mine],
             dev(wrap(yh + a, 2), x, 2 * m + zt, ct))
    own_w = local(w_ref.at[zp, :, cols(c)], rx0.at[mine])

    held_load.wait()
    plane = yh * NX + x
    own_b = []
    for i, (first, count) in enumerate(CHUNKS):
        lanes = slice(first, first + count)
        packed = jnp.dot(pick, held[:, lanes], preferred_element_type=f32).astype(bf16)
        s_b[:, :, lanes] = packed.reshape(NY * NX, 32, count)
        lanes = pl.ds(first, count)
        for a, b in planes:
            yt, xt = wrap(yh + a, 2), wrap(x + b, NX)
            send(("b", i, a, b), s_b.at[yt * NX + xt, :, lanes], r_b.at[plane, :, lanes], dev(yt, xt, z, c))
        own_b.append(local(s_b.at[plane, :, lanes], r_b.at[plane, :, lanes]))

    def piece(g, xo, dz, part=None):
        zz = wrap(z + dz, NZ)
        xx = wrap(x + xo, NX)
        kv, mm = lax.rem(zz, 2), zz // 2
        if KINDS[g] in "PQ":
            return wb.at[g, kv, yh, xx, mm]
        if part is None:
            return wb.at[g, kv, :, xx, mm]
        return wb.at[g, kv, part, xx, mm]

    def pass_on(g, way, xo, dz, part=None):
        there_x = near_x(xo - {"x+": 1, "x-": -1}.get(way, 0))
        there_z = near(dz - {"z+": 1, "z-": -1}.get(way, 0))
        there = piece(g, xo, dz, part)
        send(("w", g, there_x, there_z, part), there, there, up[way])

    def got(g, xo, dz, part=None):
        recv(("w", g, xo, dz, part), piece(g, xo, dz, part))
        if KINDS[g] in "PQ":
            cross(g, xo, dz)

    def cross(g, xo, dz):
        there = piece(g, xo, dz)
        send(("y", g, xo, dz), there, there, dev(1 - yh, x, z, c))

    def crossed(g, xo, dz):
        zz = wrap(z + dz, NZ)
        recv(("y", g, xo, dz), wb.at[g, lax.rem(zz, 2), 1 - yh, wrap(x + xo, NX), zz // 2])

    def crossed_all(g):
        if KINDS[g] not in "PQ":
            return
        for xo in (0, -1, 1, 2):
            for dz in order:
                crossed(g, xo, dz)

    own_w.wait()
    for a, b, d in flips:
        source = wrap(yh + a, 2) * 4 + wrap(zp + b, 2) * 2 + wrap(c + d, 2)
        recv(("p", a, b, d), rx0.at[source])
    for y in range(2):
        block = jnp.concatenate([rx0[y * 4 + i].astype(f32) for i in range(4)], axis=0).astype(bf16)
        for g in range(GROUPS):
            wb[g, zp, y, x, m] = block[:, g * HD : (g + 1) * HD]

    for g in range(GROUPS):
        for way in ("x+", "x-", "z+", "z-"):
            pass_on(g, way, 0, 0)
        if KINDS[g] in "PQ":
            cross(g, 0, 0)

    order = (0, -1, 1, -2, 2, -3, 3, 4)

    def x_first(g, d):
        whole = KINDS[g] == "P"
        for sign, ahead in ((-1, "z+"), (1, "z-")):
            got(g, 0, sign * d)
            if d < 3:
                pass_on(g, ahead, 0, sign * d)
            elif not whole:
                pass_on(g, ahead, 0, sign * d, 0 if sign < 0 else 1)
            elif sign < 0:
                pass_on(g, ahead, 0, sign * d)
            pass_on(g, "x+", 0, sign * d)
            pass_on(g, "x-", 0, sign * d)

    def x_first_last(g):
        if KINDS[g] == "P":
            got(g, 0, 4)
        else:
            got(g, 0, 4, 0)
            got(g, 0, 4, 1)
        pass_on(g, "x+", 0, 4)
        pass_on(g, "x-", 0, 4)

    def z_first(g):
        for sign, ahead in ((-1, "x+"), (1, "x-")):
            got(g, sign, 0)
            if sign < 0:
                pass_on(g, ahead, sign, 0)
            pass_on(g, "z+", sign, 0)
            pass_on(g, "z-", sign, 0)

    def z_first_last(g):
        got(g, 2, 0)
        pass_on(g, "z+", 2, 0)
        pass_on(g, "z-", 2, 0)

    def x_last(g, lo, hi):
        for i in range(lo, hi):
            dz = order[i]
            got(g, -1, dz)
            if i % 2 == 0:
                pass_on(g, "x+", -1, dz)
            got(g, 1, dz)
            if i % 2 == 1:
                pass_on(g, "x-", 1, dz)

    def x_end(g):
        for dz in order:
            got(g, 2, dz)

    def z_last(g, d):
        for xo in (0, -1, 1, 2):
            for sign, ahead in ((-1, "z+"), (1, "z-")):
                got(g, xo, sign * d)
                if d < 3 or (xo in (0, -1)) == (sign < 0):
                    pass_on(g, ahead, xo, sign * d)

    def z_end(g):
        for xo in (0, -1, 1, 2):
            got(g, xo, 4)

    def last(g, stage):
        if KINDS[g] in "XP":
            if stage < 3:
                x_last(g, (0, 3, 6)[stage], (3, 6, 8)[stage])
            else:
                x_end(g)
        elif stage < 3:
            z_last(g, stage + 1)
        else:
            z_end(g)

    x_chunks = [g for g in range(GROUPS) if KINDS[g] in "XP"]
    z_chunks = [g for g in range(GROUPS) if KINDS[g] in "QZ"]
    for g in x_chunks:
        x_first(g, 1)
    for g in z_chunks:
        z_first(g)

    new_i = lax.broadcasted_iota(jnp.int32, (SLOTS, SLOTS), 0)
    old_i = lax.broadcasted_iota(jnp.int32, (SLOTS, SLOTS), 1)
    wanted = lax.rem(new_i // 2, 8) * 32 + (new_i // 16) * 2 + lax.rem(new_i, 2)
    turn = jnp.where(old_i == wanted, 1.0, 0.0).astype(bf16)
    own_a = []
    for i, (first, count) in enumerate(CHUNKS):
        lanes = slice(first, first + count)
        own_b[i].wait()
        for a, b in planes:
            recv(("b", i, a, b), r_b.at[wrap(yh + a, 2) * NX + wrap(x - b, NX), :, pl.ds(first, count)])
        old = r_b[:, :, lanes].reshape(SLOTS, count)
        s_a[:, :, lanes] = jnp.dot(turn, old, preferred_element_type=f32).astype(bf16).reshape(NZ, 32, count)
        lanes = pl.ds(first, count)
        for d in (4, 3, 5, 2, 6, 1, 7):
            zt = wrap(z + d, NZ)
            send(("a", i, d), s_a.at[zt, :, lanes], xb.at[h, c, z, :, lanes], dev(yh, x, zt, c))
        own_a.append(local(s_a.at[z, :, lanes], xb.at[h, c, z, :, lanes]))

    for g in x_chunks:
        x_first(g, 2)
    for g in z_chunks:
        z_first_last(g)

    for g in x_chunks:
        x_first(g, 3)
    for g in x_chunks:
        x_first_last(g)

    doc_load.wait()
    diag = row_i == col_i
    src_iota = lax.broadcasted_iota(jnp.int32, (S, SLOTS), 0)
    slot_iota = lax.broadcasted_iota(jnp.int32, (S, SLOTS), 1)
    slot_src = (lax.rem(slot_iota // 2, 8) * NZ + lax.rem(slot_iota // 16, NZ)) * 2 + slot_iota // S
    spread = jnp.where(src_iota == slot_src, 1.0, 0.0).astype(bf16)
    ones = jnp.ones((8, S), bf16)
    slot_no = lax.rem(lax.broadcasted_iota(jnp.int32, (1, SLOTS), 1), 2).astype(f32)
    for b in range(2):
        named = jnp.where(routes[...] == chip * 2 + b, 1.0, 0.0).astype(bf16)
        counts = lax.dot_general(ones, named, (((1,), (1,)), ((), ())), preferred_element_type=f32)
        by_slot = jnp.dot(counts.astype(bf16), spread, preferred_element_type=f32)[0:1]
        bias[b, :, 0:SLOTS] = jnp.broadcast_to(jnp.where(by_slot > slot_no, 0.0, NEG), (S, SLOTS))
        q_ids = docs[pl.ds(chip * 2 + b, 1), :].astype(f32)
        q_col = jnp.sum(jnp.where(diag, q_ids, 0.0), axis=1, keepdims=True)
        for j in range(3):
            index = chip * 2 + b - 2 + j
            k_ids = docs[pl.ds(jnp.maximum(index, 0), 1), :].astype(f32)
            k_ids = jnp.where(index >= 0, k_ids, -1.0)
            fits = q_col == k_ids
            if j == 2:
                fits = fits & (col_i <= row_i)
            bias[b, :, SLOTS + j * S : SLOTS + (j + 1) * S] = jnp.where(fits, 0.0, NEG)

    def spread_rows(i):
        lanes = pl.ds(*CHUNKS[i])
        own_a[i].wait()
        for d in (4, 3, 5, 2, 6, 1, 7):
            recv(("a", i, d), xb.at[h, c, wrap(z - d, NZ), :, lanes])
        here = xb.at[h, c, :, :, lanes]
        send(("h", i), here, here, other_head)
        send(("s", i), here, here, sibling)

    def forward_rows(i):
        here = xb.at[1 - h, c, :, :, pl.ds(*CHUNKS[i])]
        recv(("h", i), here)
        send(("t", i), here, here, sibling)

    last(0, 0)
    last(1, 0)
    spread_rows(0)
    last(0, 1)
    last(1, 1)
    spread_rows(1)
    own_kv = []
    for name, ref, buf, segs in (("k", k_ref, kwb, True), ("v", v_ref, vwb, True), ("q", q_ref, qb, False), ("g", g_ref, gb, False)):
        base = 2 if segs else 0
        send((name, "s"), ref.at[:, cols(1 - c)], buf.at[seg(base + c)], sibling)
        own_kv.append(local(ref.at[:, cols(c)], buf.at[seg(base + c)]))
        if segs:
            for d in (0, 1):
                ct = wrap(c + d, 2)
                send((name, d), ref.at[:, cols(ct)], buf.at[seg(c)], (next_chip * 2 + ct, h))

    last(0, 2)
    last(1, 2)
    spread_rows(2)
    forward_rows(0)
    last(0, 3)
    last(2, 0)
    forward_rows(1)
    last(1, 3)
    last(2, 1)
    last(3, 0)
    forward_rows(2)
    last(2, 2)
    last(3, 1)
    for i in range(len(CHUNKS)):
        lanes = pl.ds(*CHUNKS[i])
        recv(("s", i), xb.at[h, 1 - c, :, :, lanes])
        recv(("t", i), xb.at[1 - h, 1 - c, :, :, lanes])
    handed = []
    nt = (((1,), (1,)), ((), ()))
    tn = (((0,), (0,)), ((), ()))
    scaling = HD ** -0.5

    def project(g):
        total = None
        for y in range(2):
            both = jnp.concatenate(
                [wb[g, kv, y].reshape(FEAT, HD) for kv in range(2)], axis=1)
            term = jnp.dot(xb[y].reshape(2 * SLOTS, FEAT), both, preferred_element_type=f32)
            total = term if total is None else total + term
        mem[0] = total[:, :HD].astype(bf16).reshape(16, 2, 16, HD)
        mem[1] = total[:, HD:].astype(bf16).reshape(16, 2, 16, HD)

    def attend(g):
        lanes = slice(g * HD, (g + 1) * HD)
        for b in range(2):
            rows = slice(b * S, (b + 1) * S)
            window = slice(b * S, b * S + 3 * S)
            query, cot = qb[rows, lanes], gb[rows, lanes]
            keys = jnp.concatenate([mem[0, :, b].reshape(SLOTS, HD), kwb[window, lanes]], axis=0)
            vals = jnp.concatenate([mem[1, :, b].reshape(SLOTS, HD), vwb[window, lanes]], axis=0)
            scores = lax.dot_general(query, keys, nt, preferred_element_type=f32) * scaling + bias[b]
            top = jnp.max(scores, axis=1, keepdims=True)
            weights = jnp.exp(scores - top)
            prob = weights * (1.0 / jnp.sum(weights, axis=1, keepdims=True))
            prob_b = prob.astype(bf16)
            out = jnp.dot(prob_b, vals, preferred_element_type=f32).astype(bf16)
            dprob = lax.dot_general(cot, vals, nt, preferred_element_type=f32)
            delta = jnp.sum(cot.astype(f32) * out.astype(f32), axis=1, keepdims=True)
            dscore = (prob * (dprob - delta) * scaling).astype(bf16)
            grad_q = jnp.dot(dscore, keys, preferred_element_type=f32).astype(bf16)
            stg[0, b, :, lanes] = out
            stg[1, b, :, lanes] = grad_q
            grad_k = lax.dot_general(dscore[:, SLOTS:], query, tn, preferred_element_type=f32)
            grad_v = lax.dot_general(prob_b[:, SLOTS:], cot, tn, preferred_element_type=f32)
            for i, grad in enumerate((grad_k, grad_v)):
                if b == 0:
                    gown[g, i, 0 : 3 * S] = grad
                else:
                    gown[g, i, S : 3 * S] += grad[: 2 * S]
                    gown[g, i, 3 * S :] = grad[2 * S :]
        for i in range(2):
            gtx[g, i] = gown[g, i, : 2 * S].astype(bf16)
        send(("e", g), gtx.at[g], grx.at[g], (prev_chip * 2 + c, h))
        hand_over(g, 0)

    def hand_over(g, first):
        lanes = pl.ds(g * HD, HD)
        there = out_ref.at[pl.ds(first, 2), :, pl.ds(pl.multiple_of(c * HALF + g * HD, HD), HD)]
        send(("o", g, first), stg.at[pl.ds(first, 2), 1 - c, :, lanes], there, sibling)
        handed.append(local(stg.at[pl.ds(first, 2), c, :, lanes], there))

    def finish(g):
        lanes = slice(g * HD, (g + 1) * HD)
        recv(("e", g), grx.at[g])
        for i in range(2):
            total = (gown[g, i, 2 * S :] + grx[g, i].astype(f32)).astype(bf16)
            for b in range(2):
                stg[2 + i, b, :, lanes] = total[b * S : (b + 1) * S]
        hand_over(g, 2)

    crossed_all(0)
    project(0)
    last(4, 0)
    last(3, 2)
    for copy in own_kv:
        copy.wait()
    recv(("k", "s"), kwb.at[seg(3 - c)])
    recv(("v", "s"), vwb.at[seg(3 - c)])
    recv(("q", "s"), qb.at[seg(1 - c)])
    recv(("g", "s"), gb.at[seg(1 - c)])
    for d in (0, 1):
        recv(("k", d), kwb.at[seg(wrap(c + d, 2))])
        recv(("v", d), vwb.at[seg(wrap(c + d, 2))])

    attend(0)
    last(4, 1)
    last(2, 3)
    crossed_all(1)
    project(1)
    last(4, 2)
    attend(1)
    crossed_all(2)
    project(2)
    attend(2)
    finish(0)
    last(3, 3)
    crossed_all(3)
    project(3)
    attend(3)
    finish(1)
    finish(2)
    last(4, 3)
    crossed_all(4)
    project(4)
    attend(4)
    finish(3)
    finish(4)
    for g in range(GROUPS):
        for first in (0, 2):
            recv(("o", g, first), out_ref.at[
                pl.ds(first, 2), :, pl.ds(pl.multiple_of((1 - c) * HALF + g * HD, HD), HD)])
    for copy in handed:
        copy.wait()
    for copy in sends:
        copy.wait_send()
    assert len(ids) <= POOL


def body(queries, keys, values, grad_out, cache, w_kv, doc_ids, routes):
    bf16, f32 = jnp.bfloat16, jnp.float32
    vmem = pl.BlockSpec(memory_space=pltpu.VMEM)
    hbm = pl.BlockSpec(memory_space=pltpu.HBM)
    result = pl.pallas_call(
        kernel,
        out_shape=jax.ShapeDtypeStruct((4, S, FEAT), bf16),
        in_specs=[hbm] * 5 + [vmem] + [hbm] * 2,
        out_specs=vmem,
        scratch_shapes=[
            pltpu.VMEM((S, S), jnp.int32),
            pltpu.VMEM((S, S), jnp.int32),
            pltpu.VMEM((S, FEAT), bf16),
            pltpu.VMEM((8, 20, HALF), bf16),
            pltpu.VMEM((GROUPS, 2, NY, NX, NZ // 2, 80, HD), bf16),
            pltpu.VMEM((NZ, 32, FEAT), bf16),
            pltpu.VMEM((NZ, 32, FEAT), bf16),
            pltpu.VMEM((NZ, 32, FEAT), bf16),
            pltpu.VMEM((2, 2, NZ, 32, FEAT), bf16),
            pltpu.VMEM((4 * S, HALF), bf16),
            pltpu.VMEM((4 * S, HALF), bf16),
            pltpu.VMEM((2 * S, HALF), bf16),
            pltpu.VMEM((2 * S, HALF), bf16),
            pltpu.VMEM((2, S, SLOTS + 3 * S), f32),
            pltpu.VMEM((2, 16, 2, 16, HD), bf16),
            pltpu.VMEM((GROUPS, 2, 2 * S, HD), bf16),
            pltpu.VMEM((GROUPS, 2, 2 * S, HD), bf16),
            pltpu.VMEM((GROUPS, 2, 4 * S, HD), f32),
            pltpu.VMEM((4, 2, S, HALF), bf16),
            pltpu.SemaphoreType.DMA((POOL,)),
            pltpu.SemaphoreType.DMA((POOL,)),
            pltpu.SemaphoreType.DMA((32,)),
        ],
        compiler_params=pltpu.CompilerParams(
            collective_id=0, has_side_effects=True, vmem_limit_bytes=64 * 2**20
        ),
        name="segment_layer",
    )(queries, keys, values, grad_out, cache, w_kv, doc_ids.reshape(S, S), routes.reshape(S, S))
    return (result[0], result[1], result[2], result[3])


def solution(mesh):
    rows = P("seq", "head")
    return jax.shard_map(
        body,
        mesh=mesh,
        in_specs=(rows, rows, rows, rows, rows, P(None, "seq", "head"), P(), P()),
        out_specs=(rows, rows, rows, rows),
        check_vma=False,
    )
```

```python
import jax
import jax.numpy as jnp
from jax import lax
from jax.experimental import pallas as pl
from jax.experimental.pallas import tpu as pltpu
from jax.sharding import PartitionSpec as P

MESH = pl.DeviceIdType.MESH
NY, NX, NZ = 2, 4, 8
HD = 128
S = 128
HALF = 640
GROUPS = 5
FEAT = 1280
SLOTS = 256
NEG = -1e30
KINDS = "XZXXX"
CHUNKS = ((0, 256), (256, 512), (768, 512))
POOL = 340


def near(offset):
    offset = offset % NZ
    return offset - NZ if offset > NZ // 2 else offset


def near_x(offset):
    offset = offset % NX
    return offset - NX if offset > NX // 2 else offset


def kernel(
    q_ref, k_ref, v_ref, g_ref, cache_ref, w_ref, doc_ref, route_ref,
    out_ref,
    routes, docs, held, rx0, wb, s_b, r_b, s_a, xb, kwb, vwb, qb, gb, bias, mem, gtx, grx, gown, stg,
    ssem, rsem, lsem,
):
    f32, bf16 = jnp.float32, jnp.bfloat16
    s = lax.axis_index("seq")
    h = lax.axis_index("head")
    c = lax.rem(s, 2)
    chip = s // 2
    z = lax.rem(chip, NZ)
    x = lax.rem(chip // NZ, NX)
    yh = chip // (NZ * NX)
    zp = lax.rem(z, 2)
    m = z // 2

    def dev(yy, xx, zz, cc, hh=None):
        return (((yy * NX + xx) * NZ + zz) * 2 + cc, h if hh is None else hh)

    def wrap(value, n):
        return lax.rem(value + 2 * n, n)

    sibling = dev(yh, x, z, 1 - c)
    other_head = (s, 1 - h)
    chips = NY * NX * NZ
    next_chip = lax.rem(chip + 1, chips)
    prev_chip = lax.rem(chip + chips - 1, chips)
    up = {"z+": dev(yh, x, wrap(z + 1, NZ), c), "z-": dev(yh, x, wrap(z - 1, NZ), c),
          "x+": dev(yh, wrap(x + 1, NX), z, c), "x-": dev(yh, wrap(x - 1, NX), z, c)}

    ids = {}
    sends = []

    def number(key):
        return ids.setdefault(key, len(ids))

    def send(key, src, dst, target):
        n = number(key)
        copy = pltpu.make_async_remote_copy(
            src_ref=src, dst_ref=dst, send_sem=ssem.at[n], recv_sem=rsem.at[n],
            device_id=target, device_id_type=MESH)
        copy.start()
        sends.append(copy)

    def recv(key, dst):
        n = number(key)
        pltpu.make_async_remote_copy(
            src_ref=dst, dst_ref=dst, send_sem=ssem.at[n], recv_sem=rsem.at[n],
            device_id=sibling, device_id_type=MESH).wait_recv()

    locals_ = []

    def local(src, dst):
        copy = pltpu.make_async_copy(src, dst, lsem.at[len(locals_)])
        copy.start()
        locals_.append(copy)
        return copy

    flips = [(a, b, d) for a in (0, 1) for b in (0, 1) for d in (0, 1) if a or b or d]
    planes = [(a, b) for a, b in ((1, 2), (0, 2), (1, 1), (1, 3), (1, 0), (0, 1), (0, 3))]

    route_load = local(route_ref, routes)
    doc_load = local(doc_ref, docs)
    held_load = local(cache_ref, held)

    barrier = pltpu.get_barrier_semaphore()
    greeted = [dev(wrap(yh + a, 2), x, 2 * m + wrap(zp + b, 2), wrap(c + d, 2)) for a, b, d in flips]
    greeted += [dev(yh, x, wrap(z + d, NZ), c) for d in range(1, NZ)]
    greeted += [dev(wrap(yh + a, 2), wrap(x + b, NX), z, c) for a, b in planes]
    greeted += [other_head]
    greeted += [(prev_chip * 2 + c, h), (prev_chip * 2 + 1 - c, h), (next_chip * 2 + c, h), (next_chip * 2 + 1 - c, h)]
    for target in greeted:
        pl.semaphore_signal(barrier, inc=1, device_id=target, device_id_type=MESH)

    def cols(core):
        return pl.ds(pl.multiple_of(core * HALF, HD), HALF)

    def seg(index):
        return pl.ds(pl.multiple_of(index * S, S), S)

    route_load.wait()
    route_own = routes[pl.ds(s, 1), :].astype(f32)
    row_i = lax.broadcasted_iota(jnp.int32, (S, S), 0)
    col_i = lax.broadcasted_iota(jnp.int32, (S, S), 1)
    route_col = jnp.sum(jnp.where(row_i == col_i, route_own, 0.0), axis=1, keepdims=True)
    same = (route_col == route_own) & (row_i < col_i)
    rank = jnp.sum(jnp.where(same, 1.0, 0.0), axis=0, keepdims=True)
    slot = lax.broadcasted_iota(jnp.int32, (SLOTS, S), 0)
    chosen = (route_own == (slot // 2).astype(f32)) & (rank == lax.rem(slot, 2).astype(f32))
    pick = jnp.where(chosen, 1.0, 0.0).astype(bf16)

    pl.semaphore_wait(barrier, len(greeted))

    mine = yh * 4 + zp * 2 + c
    for a, b, d in flips:
        zt, ct = wrap(zp + b, 2), wrap(c + d, 2)
        send(("p", a, b, d), w_ref.at[zt, :, cols(ct)], rx0.at[mine],
             dev(wrap(yh + a, 2), x, 2 * m + zt, ct))
    own_w = local(w_ref.at[zp, :, cols(c)], rx0.at[mine])

    held_load.wait()
    plane = yh * NX + x
    own_b = []
    for i, (first, count) in enumerate(CHUNKS):
        lanes = slice(first, first + count)
        packed = jnp.dot(pick, held[:, lanes], preferred_element_type=f32).astype(bf16)
        s_b[:, :, lanes] = packed.reshape(NY * NX, 32, count)
        lanes = pl.ds(first, count)
        for a, b in planes:
            yt, xt = wrap(yh + a, 2), wrap(x + b, NX)
            send(("b", i, a, b), s_b.at[yt * NX + xt, :, lanes], r_b.at[plane, :, lanes], dev(yt, xt, z, c))
        own_b.append(local(s_b.at[plane, :, lanes], r_b.at[plane, :, lanes]))

    def piece(g, xo, dz, part=None):
        zz = wrap(z + dz, NZ)
        xx = wrap(x + xo, NX)
        kv, mm = lax.rem(zz, 2), zz // 2
        if KINDS[g] in "PQ":
            return wb.at[g, kv, yh, xx, mm]
        if part is None:
            return wb.at[g, kv, :, xx, mm]
        return wb.at[g, kv, part, xx, mm]

    def pass_on(g, way, xo, dz, part=None):
        there_x = near_x(xo - {"x+": 1, "x-": -1}.get(way, 0))
        there_z = near(dz - {"z+": 1, "z-": -1}.get(way, 0))
        there = piece(g, xo, dz, part)
        send(("w", g, there_x, there_z, part), there, there, up[way])

    def got(g, xo, dz, part=None):
        recv(("w", g, xo, dz, part), piece(g, xo, dz, part))
        if KINDS[g] in "PQ":
            cross(g, xo, dz)

    def cross(g, xo, dz):
        there = piece(g, xo, dz)
        send(("y", g, xo, dz), there, there, dev(1 - yh, x, z, c))

    def crossed(g, xo, dz):
        zz = wrap(z + dz, NZ)
        recv(("y", g, xo, dz), wb.at[g, lax.rem(zz, 2), 1 - yh, wrap(x + xo, NX), zz // 2])

    def crossed_all(g):
        if KINDS[g] not in "PQ":
            return
        for xo in (0, -1, 1, 2):
            for dz in order:
                crossed(g, xo, dz)

    own_w.wait()
    for a, b, d in flips:
        source = wrap(yh + a, 2) * 4 + wrap(zp + b, 2) * 2 + wrap(c + d, 2)
        recv(("p", a, b, d), rx0.at[source])
    for y in range(2):
        block = jnp.concatenate([rx0[y * 4 + i].astype(f32) for i in range(4)], axis=0).astype(bf16)
        for g in range(GROUPS):
            wb[g, zp, y, x, m] = block[:, g * HD : (g + 1) * HD]

    for g in range(GROUPS):
        for way in ("x+", "x-", "z+", "z-"):
            pass_on(g, way, 0, 0)
        if KINDS[g] in "PQ":
            cross(g, 0, 0)

    order = (0, -1, 1, -2, 2, -3, 3, 4)

    def x_first(g, d):
        whole = KINDS[g] == "P"
        for sign, ahead in ((-1, "z+"), (1, "z-")):
            got(g, 0, sign * d)
            if d < 3:
                pass_on(g, ahead, 0, sign * d)
            elif not whole:
                pass_on(g, ahead, 0, sign * d, 0 if sign < 0 else 1)
            elif sign < 0:
                pass_on(g, ahead, 0, sign * d)
            pass_on(g, "x+", 0, sign * d)
            pass_on(g, "x-", 0, sign * d)

    def x_first_last(g):
        if KINDS[g] == "P":
            got(g, 0, 4)
        else:
            got(g, 0, 4, 0)
            got(g, 0, 4, 1)
        pass_on(g, "x+", 0, 4)
        pass_on(g, "x-", 0, 4)

    def z_first(g):
        for sign, ahead in ((-1, "x+"), (1, "x-")):
            got(g, sign, 0)
            if sign < 0:
                pass_on(g, ahead, sign, 0)
            pass_on(g, "z+", sign, 0)
            pass_on(g, "z-", sign, 0)

    def z_first_last(g):
        got(g, 2, 0)
        pass_on(g, "z+", 2, 0)
        pass_on(g, "z-", 2, 0)

    def x_last(g, lo, hi):
        for i in range(lo, hi):
            dz = order[i]
            got(g, -1, dz)
            if i % 2 == 0:
                pass_on(g, "x+", -1, dz)
            got(g, 1, dz)
            if i % 2 == 1:
                pass_on(g, "x-", 1, dz)

    def x_end(g):
        for dz in order:
            got(g, 2, dz)

    def z_last(g, d):
        for xo in (0, -1, 1, 2):
            for sign, ahead in ((-1, "z+"), (1, "z-")):
                got(g, xo, sign * d)
                if d < 3 or (xo in (0, -1)) == (sign < 0):
                    pass_on(g, ahead, xo, sign * d)

    def z_end(g):
        for xo in (0, -1, 1, 2):
            got(g, xo, 4)

    def last(g, stage):
        if KINDS[g] in "XP":
            if stage < 3:
                x_last(g, (0, 3, 6)[stage], (3, 6, 8)[stage])
            else:
                x_end(g)
        elif stage < 3:
            z_last(g, stage + 1)
        else:
            z_end(g)

    x_chunks = [g for g in range(GROUPS) if KINDS[g] in "XP"]
    z_chunks = [g for g in range(GROUPS) if KINDS[g] in "QZ"]
    for g in x_chunks:
        x_first(g, 1)
    for g in z_chunks:
        z_first(g)

    new_i = lax.broadcasted_iota(jnp.int32, (SLOTS, SLOTS), 0)
    old_i = lax.broadcasted_iota(jnp.int32, (SLOTS, SLOTS), 1)
    wanted = lax.rem(new_i // 2, 8) * 32 + (new_i // 16) * 2 + lax.rem(new_i, 2)
    turn = jnp.where(old_i == wanted, 1.0, 0.0).astype(bf16)
    own_a = []
    for i, (first, count) in enumerate(CHUNKS):
        lanes = slice(first, first + count)
        own_b[i].wait()
        for a, b in planes:
            recv(("b", i, a, b), r_b.at[wrap(yh + a, 2) * NX + wrap(x - b, NX), :, pl.ds(first, count)])
        old = r_b[:, :, lanes].reshape(SLOTS, count)
        s_a[:, :, lanes] = jnp.dot(turn, old, preferred_element_type=f32).astype(bf16).reshape(NZ, 32, count)
        lanes = pl.ds(first, count)
        for d in (4, 3, 5, 2, 6, 1, 7):
            zt = wrap(z + d, NZ)
            send(("a", i, d), s_a.at[zt, :, lanes], xb.at[h, c, z, :, lanes], dev(yh, x, zt, c))
        own_a.append(local(s_a.at[z, :, lanes], xb.at[h, c, z, :, lanes]))

    for g in x_chunks:
        x_first(g, 2)
    for g in z_chunks:
        z_first_last(g)

    for g in x_chunks:
        x_first(g, 3)
    for g in x_chunks:
        x_first_last(g)

    doc_load.wait()
    diag = row_i == col_i
    src_iota = lax.broadcasted_iota(jnp.int32, (S, SLOTS), 0)
    slot_iota = lax.broadcasted_iota(jnp.int32, (S, SLOTS), 1)
    slot_src = (lax.rem(slot_iota // 2, 8) * NZ + lax.rem(slot_iota // 16, NZ)) * 2 + slot_iota // S
    spread = jnp.where(src_iota == slot_src, 1.0, 0.0).astype(bf16)
    ones = jnp.ones((8, S), bf16)
    slot_no = lax.rem(lax.broadcasted_iota(jnp.int32, (1, SLOTS), 1), 2).astype(f32)
    for b in range(2):
        named = jnp.where(routes[...] == chip * 2 + b, 1.0, 0.0).astype(bf16)
        counts = lax.dot_general(ones, named, (((1,), (1,)), ((), ())), preferred_element_type=f32)
        by_slot = jnp.dot(counts.astype(bf16), spread, preferred_element_type=f32)[0:1]
        bias[b, :, 0:SLOTS] = jnp.broadcast_to(jnp.where(by_slot > slot_no, 0.0, NEG), (S, SLOTS))
        q_ids = docs[pl.ds(chip * 2 + b, 1), :].astype(f32)
        q_col = jnp.sum(jnp.where(diag, q_ids, 0.0), axis=1, keepdims=True)
        for j in range(3):
            index = chip * 2 + b - 2 + j
            k_ids = docs[pl.ds(jnp.maximum(index, 0), 1), :].astype(f32)
            k_ids = jnp.where(index >= 0, k_ids, -1.0)
            fits = q_col == k_ids
            if j == 2:
                fits = fits & (col_i <= row_i)
            bias[b, :, SLOTS + j * S : SLOTS + (j + 1) * S] = jnp.where(fits, 0.0, NEG)

    def spread_rows(i):
        lanes = pl.ds(*CHUNKS[i])
        own_a[i].wait()
        for d in (4, 3, 5, 2, 6, 1, 7):
            recv(("a", i, d), xb.at[h, c, wrap(z - d, NZ), :, lanes])
        here = xb.at[h, c, :, :, lanes]
        send(("h", i), here, here, other_head)
        send(("s", i), here, here, sibling)

    def forward_rows(i):
        here = xb.at[1 - h, c, :, :, pl.ds(*CHUNKS[i])]
        recv(("h", i), here)
        send(("t", i), here, here, sibling)

    last(0, 0)
    last(1, 0)
    spread_rows(0)
    own_kv = []
    for name, ref, buf, segs in (("k", k_ref, kwb, True), ("v", v_ref, vwb, True), ("q", q_ref, qb, False), ("g", g_ref, gb, False)):
        base = 2 if segs else 0
        send((name, "s"), ref.at[:, cols(1 - c)], buf.at[seg(base + c)], sibling)
        own_kv.append(local(ref.at[:, cols(c)], buf.at[seg(base + c)]))
        if segs:
            for d in (0, 1):
                ct = wrap(c + d, 2)
                send((name, d), ref.at[:, cols(ct)], buf.at[seg(c)], (next_chip * 2 + ct, h))

    last(0, 1)
    last(1, 1)
    spread_rows(1)
    last(0, 2)
    last(1, 2)
    spread_rows(2)
    forward_rows(0)
    last(0, 3)
    last(2, 0)
    forward_rows(1)
    last(1, 3)
    last(2, 1)
    last(3, 0)
    forward_rows(2)
    last(2, 2)
    last(3, 1)
    for i in range(len(CHUNKS)):
        lanes = pl.ds(*CHUNKS[i])
        recv(("s", i), xb.at[h, 1 - c, :, :, lanes])
        recv(("t", i), xb.at[1 - h, 1 - c, :, :, lanes])
    handed = []
    nt = (((1,), (1,)), ((), ()))
    tn = (((0,), (0,)), ((), ()))
    scaling = HD ** -0.5

    def project(g):
        total = None
        for y in range(2):
            both = jnp.concatenate(
                [wb[g, kv, y].reshape(FEAT, HD) for kv in range(2)], axis=1)
            term = jnp.dot(xb[y].reshape(2 * SLOTS, FEAT), both, preferred_element_type=f32)
            total = term if total is None else total + term
        mem[0] = total[:, :HD].astype(bf16).reshape(16, 2, 16, HD)
        mem[1] = total[:, HD:].astype(bf16).reshape(16, 2, 16, HD)

    def attend(g):
        lanes = slice(g * HD, (g + 1) * HD)
        for b in range(2):
            rows = slice(b * S, (b + 1) * S)
            window = slice(b * S, b * S + 3 * S)
            query, cot = qb[rows, lanes], gb[rows, lanes]
            keys = jnp.concatenate([mem[0, :, b].reshape(SLOTS, HD), kwb[window, lanes]], axis=0)
            vals = jnp.concatenate([mem[1, :, b].reshape(SLOTS, HD), vwb[window, lanes]], axis=0)
            scores = lax.dot_general(query, keys, nt, preferred_element_type=f32) * scaling + bias[b]
            top = jnp.max(scores, axis=1, keepdims=True)
            weights = jnp.exp(scores - top)
            prob = weights * (1.0 / jnp.sum(weights, axis=1, keepdims=True))
            prob_b = prob.astype(bf16)
            out = jnp.dot(prob_b, vals, preferred_element_type=f32).astype(bf16)
            dprob = lax.dot_general(cot, vals, nt, preferred_element_type=f32)
            delta = jnp.sum(cot.astype(f32) * out.astype(f32), axis=1, keepdims=True)
            dscore = (prob * (dprob - delta) * scaling).astype(bf16)
            grad_q = jnp.dot(dscore, keys, preferred_element_type=f32).astype(bf16)
            stg[0, b, :, lanes] = out
            stg[1, b, :, lanes] = grad_q
            grad_k = lax.dot_general(dscore[:, SLOTS:], query, tn, preferred_element_type=f32)
            grad_v = lax.dot_general(prob_b[:, SLOTS:], cot, tn, preferred_element_type=f32)
            for i, grad in enumerate((grad_k, grad_v)):
                if b == 0:
                    gown[g, i, 0 : 3 * S] = grad
                else:
                    gown[g, i, S : 3 * S] += grad[: 2 * S]
                    gown[g, i, 3 * S :] = grad[2 * S :]
        for i in range(2):
            gtx[g, i] = gown[g, i, : 2 * S].astype(bf16)
        send(("e", g), gtx.at[g], grx.at[g], (prev_chip * 2 + c, h))
        hand_over(g, 0)

    def hand_over(g, first):
        lanes = pl.ds(g * HD, HD)
        there = out_ref.at[pl.ds(first, 2), :, pl.ds(pl.multiple_of(c * HALF + g * HD, HD), HD)]
        send(("o", g, first), stg.at[pl.ds(first, 2), 1 - c, :, lanes], there, sibling)
        handed.append(local(stg.at[pl.ds(first, 2), c, :, lanes], there))

    def finish(g):
        lanes = slice(g * HD, (g + 1) * HD)
        recv(("e", g), grx.at[g])
        for i in range(2):
            total = (gown[g, i, 2 * S :] + grx[g, i].astype(f32)).astype(bf16)
            for b in range(2):
                stg[2 + i, b, :, lanes] = total[b * S : (b + 1) * S]
        hand_over(g, 2)

    crossed_all(0)
    project(0)
    last(4, 0)
    last(3, 2)
    for copy in own_kv:
        copy.wait()
    recv(("k", "s"), kwb.at[seg(3 - c)])
    recv(("v", "s"), vwb.at[seg(3 - c)])
    recv(("q", "s"), qb.at[seg(1 - c)])
    recv(("g", "s"), gb.at[seg(1 - c)])
    for d in (0, 1):
        recv(("k", d), kwb.at[seg(wrap(c + d, 2))])
        recv(("v", d), vwb.at[seg(wrap(c + d, 2))])

    attend(0)
    last(4, 1)
    last(2, 3)
    crossed_all(1)
    project(1)
    last(4, 2)
    attend(1)
    crossed_all(2)
    project(2)
    attend(2)
    finish(0)
    last(3, 3)
    crossed_all(3)
    project(3)
    attend(3)
    finish(1)
    finish(2)
    last(4, 3)
    crossed_all(4)
    project(4)
    attend(4)
    finish(3)
    finish(4)
    for g in range(GROUPS):
        for first in (0, 2):
            recv(("o", g, first), out_ref.at[
                pl.ds(first, 2), :, pl.ds(pl.multiple_of((1 - c) * HALF + g * HD, HD), HD)])
    for copy in handed:
        copy.wait()
    for copy in sends:
        copy.wait_send()
    assert len(ids) <= POOL


def body(queries, keys, values, grad_out, cache, w_kv, doc_ids, routes):
    bf16, f32 = jnp.bfloat16, jnp.float32
    vmem = pl.BlockSpec(memory_space=pltpu.VMEM)
    hbm = pl.BlockSpec(memory_space=pltpu.HBM)
    result = pl.pallas_call(
        kernel,
        out_shape=jax.ShapeDtypeStruct((4, S, FEAT), bf16),
        in_specs=[hbm] * 5 + [vmem] + [hbm] * 2,
        out_specs=vmem,
        scratch_shapes=[
            pltpu.VMEM((S, S), jnp.int32),
            pltpu.VMEM((S, S), jnp.int32),
            pltpu.VMEM((S, FEAT), bf16),
            pltpu.VMEM((8, 20, HALF), bf16),
            pltpu.VMEM((GROUPS, 2, NY, NX, NZ // 2, 80, HD), bf16),
            pltpu.VMEM((NZ, 32, FEAT), bf16),
            pltpu.VMEM((NZ, 32, FEAT), bf16),
            pltpu.VMEM((NZ, 32, FEAT), bf16),
            pltpu.VMEM((2, 2, NZ, 32, FEAT), bf16),
            pltpu.VMEM((4 * S, HALF), bf16),
            pltpu.VMEM((4 * S, HALF), bf16),
            pltpu.VMEM((2 * S, HALF), bf16),
            pltpu.VMEM((2 * S, HALF), bf16),
            pltpu.VMEM((2, S, SLOTS + 3 * S), f32),
            pltpu.VMEM((2, 16, 2, 16, HD), bf16),
            pltpu.VMEM((GROUPS, 2, 2 * S, HD), bf16),
            pltpu.VMEM((GROUPS, 2, 2 * S, HD), bf16),
            pltpu.VMEM((GROUPS, 2, 4 * S, HD), f32),
            pltpu.VMEM((4, 2, S, HALF), bf16),
            pltpu.SemaphoreType.DMA((POOL,)),
            pltpu.SemaphoreType.DMA((POOL,)),
            pltpu.SemaphoreType.DMA((32,)),
        ],
        compiler_params=pltpu.CompilerParams(
            collective_id=0, has_side_effects=True, vmem_limit_bytes=64 * 2**20
        ),
        name="segment_layer",
    )(queries, keys, values, grad_out, cache, w_kv, doc_ids.reshape(S, S), routes.reshape(S, S))
    return (result[0], result[1], result[2], result[3])


def solution(mesh):
    rows = P("seq", "head")
    return jax.shard_map(
        body,
        mesh=mesh,
        in_specs=(rows, rows, rows, rows, rows, P(None, "seq", "head"), P(), P()),
        out_specs=(rows, rows, rows, rows),
        check_vma=False,
    )
```
